32 devices in a mesh: rep: 8 (over y, x, core), grp: 4 (over z).
Axes of the slice: x: 2, y: 2, z: 4, core: 2. Of those that a mesh axis runs over, the one named last changes fastest.
Arguments:
- layer_input: bfloat16 [8, 1024, 2048], P('rep', 'grp'), may hold values from -6 to 6
- w_qkv: bfloat16 [2048, 1920], P('grp'), may hold values from -0.125 to 0.125
- w_out: bfloat16 [1280, 2048], P('grp'), may hold values from -2.5 to 2.5
- w_in: bfloat16 [5120, 2, 2048], P('grp'), may hold values from -0.125 to 0.125
- w_down: bfloat16 [5120, 2048], P('grp'), may hold values from -0.078125 to 0.078125
- attn_gain: float32 [2048], replicated, may hold values from 0.1 to 1.9
- ffn_gain: float32 [2048], replicated, may hold values from 0.1 to 1.9
- q_gain: float32 [64], replicated, may hold values from 0.1 to 1.9
- k_gain: float32 [64], replicated, may hold values from 0.1 to 1.9
- cotangent: bfloat16 [8, 1024, 2048], P('rep', 'grp'), may hold values from -6 to 6
- prefix_len: int32 [8], replicated, may hold values from 102 to 512, as said below
- seq_slot: int32 [8], P('rep'), may hold values from 0 to 7, each once
Outputs:
- layer_output: bfloat16 [8, 1024, 2048], P('rep', 'grp')
- input_grad: float32 [8, 1024, 2048], P('rep', 'grp')
- d_w_qkv: float32 [2048, 1920], P('grp')
- d_w_out: float32 [1280, 2048], P('grp')
- d_w_in: float32 [5120, 2, 2048], P('grp')
- d_w_down: float32 [5120, 2048], P('grp')
- d_attn_gain: float32 [2048], replicated
- d_ffn_gain: float32 [2048], replicated
- d_q_gain: float32 [64], replicated
- d_k_gain: float32 [64], replicated
The draws below stay inside these ranges and needn't reach their ends.
Inputs may be any that keep to these rules, and one draw needn't show every extreme that they name: `prefix_len`: prefix length of each sequence; both ends of the range are taken by some sequence. `seq_slot`: a permutation of the sequence numbers 0 to 7.
All inputs are finite; a program needn't handle non-finite values.
Results may differ from the reference program's by a relative error of at most 0.015.
The reference program's roundings to bfloat16 on the way count: a program that leaves them out, or rounds other values in their place, can miss the bound.
Values may be sent and summed in bfloat16 or wider, within the bound.
No kernel may reach another device: no remote copies, remote signals or barrier semaphores. Data moves between devices by JAX's collectives and lax.ppermute only.
A program may use at most 256 MiB of HBM per device.

```python
import jax
import jax.numpy as jnp
from jax import lax

D = 2048
QUERY_HEADS = 20
KEY_VALUE_HEADS = 5
HEAD_SIZE = 64
FF = 5120
LENGTH = 1024
SEQS = 8
QKV = 1920


def draw_prefix_len(key, part):
    low_mark = LENGTH // 10
    high_mark = LENGTH // 2
    key_values, key_top, key_offset = jax.random.split(jax.random.fold_in(key, 17), 3)
    values_drawn = jax.random.randint(key_values, (SEQS,), low_mark, high_mark + 1)
    top_index = jax.random.randint(key_top, (), 0, SEQS)
    offset_step = jax.random.randint(key_offset, (), 1, SEQS)
    bottom_index = (top_index + offset_step) % SEQS
    positions = jnp.arange(SEQS)
    values_drawn = jnp.where(positions == top_index, high_mark, values_drawn)
    values_drawn = jnp.where(positions == bottom_index, low_mark, values_drawn)
    return values_drawn.astype(jnp.int32)


def with_spikes(array, stream_key, source, target, parts, factor):
    def block_of(dim):
        return (jnp.arange(array.shape[dim]) // (array.shape[dim] // parts)).reshape((-1,) + (1,) * (array.ndim - 1 - dim))

    near = jax.random.permutation(stream_key, parts)[block_of(target)]
    far = (block_of(target) + parts // 2) % parts
    return jnp.where((block_of(source) == near) | (block_of(source) == far), factor * array, array)


def steps_of(rng, extent, cuts, low, top_value):
    level, own = 1.0, jax.random.fold_in(rng, 6)
    for axis_at, parts in cuts:
        steps = jnp.exp(jax.random.uniform(jax.random.fold_in(own, axis_at), (parts,), jnp.float32, low / len(cuts), top_value / len(cuts)))
        level = level * jnp.repeat(steps, extent[axis_at] // parts).reshape([-1 if axis == axis_at else 1 for axis in range(len(extent))])
    return level


def gaussian(stream_key, dims, scale, bound, pieces=(), kind=jnp.bfloat16):
    drawn = scale * jax.random.normal(stream_key, dims, jnp.float32)
    if pieces:
        drawn = drawn * steps_of(stream_key, dims, pieces, -0.22, 0.18)
    return jnp.clip(drawn, -bound, bound).astype(kind)


def heavy_noise(rng, shape, width, most, cuts, heavy, kind=jnp.bfloat16):
    values = width * jax.random.normal(rng, shape, jnp.float32)
    if cuts:
        values = values * steps_of(rng, shape, cuts, -0.22, 0.18)
    return jnp.clip(with_spikes(values, jax.random.fold_in(rng, 3), *heavy), -most, most).astype(kind)


def setup_inputs(seed: int = 0) -> dict:
    streams_of = jax.random.split(jax.random.key(seed), 13)
    layer_input = heavy_noise(streams_of[0], (SEQS, LENGTH, D), 1.0, 6.0, ((0, 8), (1, 4)), (1, 2, 4, 2.0))
    w_qkv = gaussian(streams_of[1], (D, QKV), D ** -0.5, 0.125, ((0, 4),))
    w_out = gaussian(streams_of[2], (QUERY_HEADS * HEAD_SIZE, D), (max(1, QUERY_HEADS * HEAD_SIZE * 4 // LENGTH)) ** -0.5, 2.5, ((0, 4),))
    w_in = gaussian(streams_of[3], (FF, 2, D), D ** -0.5, 0.125, ((0, 4),))
    w_down = gaussian(streams_of[4], (FF, D), FF ** -0.5, 0.078125, ((0, 4),))
    attn_gain = jnp.clip(1.0 + 0.18 * jax.random.normal(streams_of[5], (D,), jnp.float32), 0.1, 1.9)
    ffn_gain = jnp.clip(1.0 + 0.18 * jax.random.normal(streams_of[6], (D,), jnp.float32), 0.1, 1.9)
    q_gain = jnp.clip(1.0 + 0.18 * jax.random.normal(streams_of[7], (HEAD_SIZE,), jnp.float32), 0.1, 1.9)
    k_gain = jnp.clip(1.0 + 0.18 * jax.random.normal(streams_of[8], (HEAD_SIZE,), jnp.float32), 0.1, 1.9)
    cotangent = gaussian(streams_of[9], (SEQS, LENGTH, D), 1.0, 6.0, ((0, 8), (1, 4)))
    prefix_len = draw_prefix_len(jax.random.fold_in(streams_of[12], 71), 0)
    seq_slot = jax.random.permutation(streams_of[11], SEQS).astype(jnp.int32)
    return dict(layer_input=layer_input, w_qkv=w_qkv, w_out=w_out, w_in=w_in, w_down=w_down, attn_gain=attn_gain, ffn_gain=ffn_gain, q_gain=q_gain, k_gain=k_gain, cotangent=cotangent, prefix_len=prefix_len, seq_slot=seq_slot)


NORM_EPSILON = 1e-06
ROPE_THETA = 10000.0
MASK_FLOOR = -1e+30
EXACT_PRECISION = lax.Precision.HIGHEST

@jax.custom_vjp
def low(v):
    return lax.optimization_barrier(v.astype(jnp.bfloat16)).astype(jnp.float32)

@jax.custom_vjp
def low_back(v):
    return v

def low_keep(v):
    return (low(v), None)

def low_pass(kept, grad):
    return (grad,)

def back_keep(v):
    return (v, None)

def back_low(kept, grad):
    return (low(grad),)
low.defvjp(low_keep, low_pass)
low_back.defvjp(back_keep, back_low)

def rope_tables(positions):
    half_dim = HEAD_SIZE // 2
    freqs = ROPE_THETA ** (-(2.0 * jnp.arange(half_dim, dtype=jnp.float32)) / HEAD_SIZE)
    angles = positions.astype(jnp.float32)[:, None] * freqs[None, :]
    return (jnp.cos(angles), jnp.sin(angles))

def rotate(values, cos_table, sin_table):
    half_dim = values.shape[-1] // 2
    first_half = values[..., :half_dim]
    second_half = values[..., half_dim:]
    cos_b = cos_table[:, None, :]
    sin_b = sin_table[:, None, :]
    return jnp.concatenate([first_half * cos_b - second_half * sin_b, second_half * cos_b + first_half * sin_b], axis=-1)

def head_scale(values, gain):
    return values * lax.rsqrt(lax.optimization_barrier(jnp.mean(values * values, axis=-1, keepdims=True)) + NORM_EPSILON) * gain

def block_forward(inputs, w_qkv, w_out, w_in, w_down, attn_gain, ffn_gain, q_gain, k_gain, prefix):
    sequence_length = inputs.shape[0]
    query_width = QUERY_HEADS * HEAD_SIZE
    key_value_width = KEY_VALUE_HEADS * HEAD_SIZE
    group_width = QUERY_HEADS // KEY_VALUE_HEADS
    inv_one = lax.rsqrt(lax.optimization_barrier(jnp.mean(inputs * inputs, axis=-1, keepdims=True)) + NORM_EPSILON)
    xn_low = low(inputs * inv_one * attn_gain)
    query_key_value = low_back(jnp.dot(xn_low, w_qkv, precision=EXACT_PRECISION))
    queries = query_key_value[:, :query_width].reshape(sequence_length, QUERY_HEADS, HEAD_SIZE)
    key_row_block = query_key_value[:, query_width:query_width + key_value_width].reshape(sequence_length, KEY_VALUE_HEADS, HEAD_SIZE)
    value_row_block = query_key_value[:, query_width + key_value_width:].reshape(sequence_length, KEY_VALUE_HEADS, HEAD_SIZE)
    positions = jnp.arange(sequence_length, dtype=jnp.int32)
    cos_table, sin_table = rope_tables(positions)
    query_lowered = low(rotate(head_scale(queries, q_gain), cos_table, sin_table))
    k_low = low(rotate(head_scale(key_row_block, k_gain), cos_table, sin_table))
    v_low = low(value_row_block)
    head_queries = query_lowered.reshape(sequence_length, KEY_VALUE_HEADS, group_width, HEAD_SIZE).transpose(1, 2, 0, 3)
    head_keys = k_low.transpose(1, 0, 2)
    head_values = v_low.transpose(1, 0, 2)
    allowed = (positions[None, :] <= positions[:, None]) | (positions[None, :] < prefix)

    def one_head(operands):
        head_q, head_k, head_v = operands
        scores = jnp.einsum('gqd,kd->gqk', head_q, head_k, precision=EXACT_PRECISION) * HEAD_SIZE ** (-0.5)
        scores = low_back(scores)
        scores = jnp.where(allowed[None], scores, MASK_FLOOR)
        row_top = lax.optimization_barrier(jnp.max(scores, axis=-1, keepdims=True))
        exp_scores = jnp.exp(scores - row_top)
        probabilities = low(exp_scores / lax.optimization_barrier(jnp.sum(exp_scores, axis=-1, keepdims=True)))
        return jnp.einsum('gqk,kd->gqd', probabilities, head_v, precision=EXACT_PRECISION)
    attn_heads = lax.map(jax.checkpoint(one_head), (head_queries, head_keys, head_values))
    attn_low = low(low_back(attn_heads.transpose(2, 0, 1, 3).reshape(sequence_length, query_width)))
    hidden = inputs + low_back(jnp.dot(attn_low, w_out, precision=EXACT_PRECISION))
    inv_two = lax.rsqrt(lax.optimization_barrier(jnp.mean(hidden * hidden, axis=-1, keepdims=True)) + NORM_EPSILON)
    hn_low = low(hidden * inv_two * ffn_gain)
    projected = low_back(jnp.einsum('td,fgd->tgf', hn_low, w_in, precision=EXACT_PRECISION))
    mixed_low = low(jax.nn.silu(projected[:, 0]) * projected[:, 1])
    return hidden + low_back(jnp.dot(mixed_low, w_down, precision=EXACT_PRECISION))

def add_terms(running, term_one):
    return running + term_one

def reference(layer_input, w_qkv, w_out, w_in, w_down, attn_gain, ffn_gain, q_gain, k_gain, cotangent, prefix_len, seq_slot):
    params = (w_qkv.astype(jnp.float32), w_out.astype(jnp.float32), w_in.astype(jnp.float32), w_down.astype(jnp.float32), attn_gain.astype(jnp.float32), ffn_gain.astype(jnp.float32), q_gain.astype(jnp.float32), k_gain.astype(jnp.float32))
    slot_ids = jnp.arange(SEQS, dtype=jnp.int32)
    prefixes = lax.optimization_barrier(jnp.sum(jnp.where(seq_slot[:, None] == slot_ids[None, :], prefix_len[None, :], 0), axis=1)).astype(jnp.int32)

    def per_sequence(running, entries):
        inputs_low, grad_low, prefix = entries

        def forward(inputs_f, weights):
            return block_forward(inputs_f, weights[0], weights[1], weights[2], weights[3], weights[4], weights[5], weights[6], weights[7], prefix)
        result, pullback = jax.vjp(forward, inputs_low.astype(jnp.float32), params)
        grad_inputs_one, grad_params = pullback(grad_low.astype(jnp.float32))
        running = jax.tree.map(add_terms, running, grad_params)
        return (running, (result.astype(jnp.bfloat16), grad_inputs_one))
    zero_grads = jax.tree.map(jnp.zeros_like, params)
    totals, (outputs, grad_inputs) = lax.scan(per_sequence, zero_grads, (layer_input, cotangent, prefixes))
    return (outputs, grad_inputs, totals[0], totals[1], totals[2], totals[3], totals[4], totals[5], totals[6], totals[7])
```

```python
import functools

import jax
import jax.numpy as jnp
from jax import lax
from jax.experimental import pallas as pl
from jax.experimental.pallas import tpu as pltpu
from jax.sharding import PartitionSpec as P

QUERY_HEADS = 20
KEY_VALUE_HEADS = 5
HEAD_SIZE = 64
GROUP = QUERY_HEADS // KEY_VALUE_HEADS
QUERY_WIDTH = QUERY_HEADS * HEAD_SIZE
KEY_VALUE_WIDTH = KEY_VALUE_HEADS * HEAD_SIZE
NORM_EPSILON = 1e-06
ROPE_THETA = 10000.0
LOG2E = 1.4426950408889634
BF = jnp.bfloat16
F32 = jnp.float32


def dot(a, b, ca, cb):
    return lax.dot_general(a, b, (((ca,), (cb,)), ((), ())), preferred_element_type=F32)


def rep_orders():
    bits = lax.axis_size("rep").bit_length() - 1
    rest = list(range(1, bits))
    return [0] + rest, [0] + rest[::-1]


def bit_of(b):
    return (lax.axis_index("rep") >> b) & 1


def swap(x, b):
    n = lax.axis_size("rep")
    return lax.ppermute(x, "rep", [(i, i ^ (1 << b)) for i in range(n)])


def place_of(order):
    place = 0
    for b in order:
        place = place * 2 + bit_of(b)
    return place


def rep_scatter(x, order, axis):
    for b in order:
        half = x.shape[axis] // 2
        bit = bit_of(b)
        away = lax.dynamic_slice_in_dim(x, (1 - bit) * half, half, axis).astype(BF)
        keep = lax.dynamic_slice_in_dim(x, bit * half, half, axis)
        x = keep.astype(F32) + swap(away, b).astype(F32)
    return x


def rep_gather(x, order, axis):
    for b in order[::-1]:
        other = swap(x, b)
        x = jnp.where(
            bit_of(b) == 0,
            jnp.concatenate([x, other], axis),
            jnp.concatenate([other, x], axis),
        )
    return x


EDGE = [(0, 1), (1, 0), (2, 3), (3, 2)]
MID = [(1, 2), (2, 1)]
OUTWARD = [(1, 0), (2, 3)]
INWARD = [(0, 1), (3, 2)]


def ring(n):
    return [(i, (i + 1) % n) for i in range(n)]


def slot_sources():
    n = lax.axis_size("grp")
    g = lax.axis_index("grp")
    if n == 4:
        return [g, g ^ 1, jnp.where(g < 2, 2, 1), jnp.where(g < 2, 3, 0)]
    return [lax.rem(g + n - k, n) for k in range(n)]


def spread(x):
    n = lax.axis_size("grp")
    if n == 4:
        g = lax.axis_index("grp")
        middle = (g == 1) | (g == 2)
        p1 = lax.ppermute(x, "grp", EDGE)
        p2 = lax.ppermute(x, "grp", MID)
        p3 = lax.ppermute(p1, "grp", MID)
        p4 = lax.ppermute(p2, "grp", OUTWARD)
        p5 = lax.ppermute(p3, "grp", OUTWARD)
        return [x, p1, jnp.where(middle, p2, p4), jnp.where(middle, p3, p5)]
    slots = [x]
    for _ in range(n - 1):
        slots.append(lax.ppermute(slots[-1], "grp", ring(n)))
    return slots


def collect(parts):
    n = lax.axis_size("grp")

    def send(x, pairs):
        return lax.ppermute(x.astype(BF), "grp", pairs).astype(F32)

    if n == 4:
        q1 = send(parts[3], INWARD)
        q2 = send(parts[3] + q1, MID)
        q3 = send(parts[2], INWARD)
        q4 = send(parts[2] + q3, MID)
        q5 = send(parts[1] + q2, EDGE)
        return parts[0] + q4 + q5
    total = parts[1]
    for k in list(range(2, n)) + [0]:
        total = send(total, ring(n)) + parts[k]
    return total


def fetch_shards(w, axis):
    n = lax.axis_size("grp")
    g = lax.axis_index("grp")
    orders = rep_orders()
    half = w.shape[axis] // 2
    size = half // lax.axis_size("rep")
    pieces = [
        lax.dynamic_slice_in_dim(w, i * half + place_of(order) * size, size, axis)
        for i, order in enumerate(orders)
    ]
    mine = jnp.stack(pieces)
    shards = []
    for k in range(1, n):
        there = lax.ppermute(mine, "grp", [(i, (i + k) % n) for i in range(n)])
        shards.append(there)
    there = jnp.stack(shards, 1)
    halves = [rep_gather(there[i], order, axis + 1) for i, order in enumerate(orders)]
    whole = jnp.concatenate(halves, axis + 1)
    return [(lax.rem(g + n - k, n), whole[k - 1]) for k in range(1, n)]


def assemble(w, shards):
    g = lax.axis_index("grp")
    rows = w.shape[0]
    full = jnp.zeros((rows * lax.axis_size("grp"), w.shape[1]), w.dtype)
    for source, shard in [(g, w)] + shards:
        full = lax.dynamic_update_slice_in_dim(full, shard, source * rows, 0)
    return full


def sum_everywhere(x):
    for b in range(lax.axis_size("rep").bit_length() - 1):
        x = x + swap(x, b)
    n = lax.axis_size("grp")
    for b in range(n.bit_length() - 1):
        x = x + lax.ppermute(x, "grp", [(i, i ^ (1 << b)) for i in range(n)])
    return x


def mask_limit(info_ref, tokens):
    query_pos = info_ref[1] + lax.broadcasted_iota(jnp.int32, (1, tokens), 1)
    return jnp.maximum(query_pos + 1, info_ref[0])


def forward_kernel(info_ref, q_ref, k_ref, v_ref, o_ref, of_ref, inv_ref):
    slots, _, tokens = k_ref.shape
    limit = mask_limit(info_ref, tokens)
    for h in range(GROUP):
        rows = slice(h * HEAD_SIZE, (h + 1) * HEAD_SIZE)
        q = q_ref[rows, :]
        total = jnp.zeros((1, tokens), F32)
        acc = jnp.zeros((HEAD_SIZE, tokens), F32)
        for s in range(slots):
            key_pos = info_ref[2 + s] + lax.broadcasted_iota(jnp.int32, (tokens, tokens), 0)
            t = dot(k_ref[s], q, 0, 0) * (HEAD_SIZE**-0.5 * LOG2E)
            e = jnp.where(key_pos < limit, jnp.exp2(t), 0.0)
            total = total + jnp.sum(e, axis=0, keepdims=True)
            acc = acc + dot(v_ref[s], e.astype(BF), 1, 0)
        inv = 1.0 / total
        out = acc * inv
        o_ref[rows, :] = out.astype(BF)
        of_ref[rows, :] = out
        inv_ref[0, h : h + 1, :] = inv


def backward_kernel(info_ref, q_ref, k_ref, v_ref, g_ref, of_ref, inv_ref, dq_ref, dk_ref, dv_ref):
    slots, _, tokens = k_ref.shape
    limit = mask_limit(info_ref, tokens)
    for h in range(GROUP):
        rows = slice(h * HEAD_SIZE, (h + 1) * HEAD_SIZE)
        q = q_ref[rows, :]
        grad = g_ref[rows, :]
        inv = inv_ref[0, h : h + 1, :]
        delta = jnp.sum(of_ref[rows, :] * grad.astype(F32), axis=0, keepdims=True)
        acc = jnp.zeros((HEAD_SIZE, tokens), F32)
        for s in range(slots):
            key_pos = info_ref[2 + s] + lax.broadcasted_iota(jnp.int32, (tokens, tokens), 0)
            t = dot(k_ref[s], q, 0, 0) * (HEAD_SIZE**-0.5 * LOG2E)
            p = jnp.where(key_pos < limit, jnp.exp2(t) * inv, 0.0)
            dp = dot(v_ref[s], grad, 0, 0)
            ds = (p * (dp - delta)).astype(BF)
            acc = acc + dot(k_ref[s], ds, 1, 0)
            dk = dot(q, ds, 1, 1) * HEAD_SIZE**-0.5
            dv = dot(grad, p.astype(BF), 1, 1)
            if h == 0:
                dk_ref[s] = dk
                dv_ref[s] = dv
            else:
                dk_ref[s] += dk
                dv_ref[s] += dv
        dq_ref[rows, :] = acc * HEAD_SIZE**-0.5


def attention_specs(slots, tokens):
    heads = pl.BlockSpec((GROUP * HEAD_SIZE, tokens), lambda c, info: (c, 0))
    keys = pl.BlockSpec((slots, HEAD_SIZE, tokens), lambda c, info: (0, c, 0))
    values = pl.BlockSpec((slots, HEAD_SIZE, tokens), lambda c, info: (0, KEY_VALUE_HEADS + c, 0))
    inverse = pl.BlockSpec((1, GROUP, tokens), lambda c, info: (c, 0, 0))
    return heads, keys, values, inverse


def attention_forward(info, q, kv):
    slots, _, tokens = kv.shape
    heads, keys, values, inverse = attention_specs(slots, tokens)
    return pl.pallas_call(
        forward_kernel,
        grid_spec=pltpu.PrefetchScalarGridSpec(
            num_scalar_prefetch=1,
            grid=(KEY_VALUE_HEADS,),
            in_specs=[heads, keys, values],
            out_specs=[heads, heads, inverse],
        ),
        out_shape=[
            jax.ShapeDtypeStruct((QUERY_WIDTH, tokens), BF),
            jax.ShapeDtypeStruct((QUERY_WIDTH, tokens), F32),
            jax.ShapeDtypeStruct((KEY_VALUE_HEADS, GROUP, tokens), F32),
        ],
        compiler_params=pltpu.CompilerParams(vmem_limit_bytes=48 * 2**20),
        cost_estimate=pl.CostEstimate(
            flops=16 * slots * tokens * tokens * QUERY_WIDTH,
            bytes_accessed=8 * QUERY_WIDTH * tokens,
            transcendentals=QUERY_HEADS * slots * tokens * tokens,
        ),
        name="attention_forward",
    )(info, q, kv, kv)


def attention_backward(info, q, kv, grad, of, inv):
    slots, _, tokens = kv.shape
    heads, keys, values, inverse = attention_specs(slots, tokens)
    return pl.pallas_call(
        backward_kernel,
        grid_spec=pltpu.PrefetchScalarGridSpec(
            num_scalar_prefetch=1,
            grid=(KEY_VALUE_HEADS,),
            in_specs=[heads, keys, values, heads, heads, inverse],
            out_specs=[heads, keys, keys],
        ),
        out_shape=[
            jax.ShapeDtypeStruct((QUERY_WIDTH, tokens), F32),
            jax.ShapeDtypeStruct((slots, KEY_VALUE_WIDTH, tokens), F32),
            jax.ShapeDtypeStruct((slots, KEY_VALUE_WIDTH, tokens), F32),
        ],
        compiler_params=pltpu.CompilerParams(vmem_limit_bytes=48 * 2**20),
        cost_estimate=pl.CostEstimate(
            flops=40 * slots * tokens * tokens * QUERY_WIDTH,
            bytes_accessed=16 * QUERY_WIDTH * tokens,
            transcendentals=QUERY_HEADS * slots * tokens * tokens,
        ),
        name="attention_backward",
    )(info, q, kv, kv, grad, of, inv)


def inverse_rms(values, axis):
    return lax.rsqrt(jnp.mean(values * values, axis=axis, keepdims=True) + NORM_EPSILON)


def norm_back(grad_out, normed, inv_scale, gain, axis):
    scaled = grad_out * gain
    return inv_scale * (scaled - normed * jnp.mean(scaled * normed, axis=axis, keepdims=True))


def rotate(values, cos_t, sin_t, sign):
    half = HEAD_SIZE // 2
    first, second = values[:, :half], values[:, half:]
    sin_t = sin_t * sign
    return jnp.concatenate([first * cos_t - second * sin_t, second * cos_t + first * sin_t], axis=1)


def per_device(
    layer_input,
    w_qkv,
    w_out,
    w_in,
    w_down,
    attn_gain,
    ffn_gain,
    q_gain,
    k_gain,
    cotangent,
    prefix_len,
    seq_slot,
):
    xf = layer_input[0].astype(F32)
    tokens, width = xf.shape
    g = lax.axis_index("grp")
    sources = slot_sources()
    positions = g * tokens + jnp.arange(tokens, dtype=jnp.int32)
    slot_ids = jnp.arange(prefix_len.shape[0], dtype=jnp.int32)
    prefix = jnp.sum(jnp.where(slot_ids == seq_slot[0], prefix_len, 0))
    info = jnp.stack([prefix, g * tokens] + [s * tokens for s in sources]).astype(jnp.int32)
    half = HEAD_SIZE // 2
    freqs = ROPE_THETA ** (-(2.0 * jnp.arange(half, dtype=F32)) / HEAD_SIZE)
    angles = freqs[:, None] * positions.astype(F32)[None, :]
    cos_t, sin_t = jnp.cos(angles), jnp.sin(angles)
    w_gate, w_up = w_in[:, 0], w_in[:, 1]

    inv_one = inverse_rms(xf, 1)
    normed_one = xf * inv_one
    xn = (normed_one * attn_gain).astype(BF)

    w_kv, w_q = w_qkv[:, QUERY_WIDTH:], w_qkv[:, :QUERY_WIDTH]
    kv_shards = fetch_shards(w_kv, 0)
    q_shards = fetch_shards(w_q, 0)
    out_shards = fetch_shards(w_out, 1)
    rows = w_qkv.shape[0]

    def project(own, shards):
        total = 0.0
        for source, shard in [(g, own)] + shards:
            total = total + dot(
                shard, lax.dynamic_slice_in_dim(xn, source * rows, rows, 1), 0, 1
            )
        return total

    kv_t = project(w_kv, kv_shards)
    k_raw = kv_t[:KEY_VALUE_WIDTH].reshape(KEY_VALUE_HEADS, HEAD_SIZE, tokens)
    k_inv = inverse_rms(k_raw, 1)
    k_normed = k_raw * k_inv
    k_low = rotate(k_normed * k_gain[:, None], cos_t, sin_t, 1.0).astype(BF)
    local_kv = jnp.concatenate(
        [k_low.reshape(KEY_VALUE_WIDTH, tokens), kv_t[KEY_VALUE_WIDTH:].astype(BF)], 0
    )
    kv = jnp.stack(spread(local_kv))
    q_t = project(w_q, q_shards)
    q_raw = q_t.reshape(QUERY_HEADS, HEAD_SIZE, tokens)
    q_inv = inverse_rms(q_raw, 1)
    q_normed = q_raw * q_inv
    q_low = rotate(q_normed * q_gain[:, None], cos_t, sin_t, 1.0).astype(BF)
    q_low = q_low.reshape(QUERY_WIDTH, tokens)

    ob, of, soft_inv = attention_forward(info, q_low, kv)
    w_out_full = assemble(w_out, out_shards)
    hid = xf + dot(ob, w_out_full, 0, 0)
    inv_two = inverse_rms(hid, 1)
    normed_two = hid * inv_two
    hn = (normed_two * ffn_gain).astype(BF)

    dy = cotangent[0]
    dy_slots = spread(dy)
    hn_slots = spread(hn)
    m_slots, dg_slots, du_slots, dhn_parts, out_parts = [], [], [], [], []
    for hn_s, dy_s in zip(hn_slots, dy_slots):
        gate = dot(hn_s, w_gate, 1, 1)
        up = dot(hn_s, w_up, 1, 1)
        dm = dot(dy_s, w_down, 1, 1)
        sg = jax.nn.sigmoid(gate)
        act = gate * sg
        m_s = (act * up).astype(BF)
        dg_s = (dm * up * sg * (1.0 + gate * (1.0 - sg))).astype(BF)
        du_s = (dm * act).astype(BF)
        m_slots.append(m_s)
        dg_slots.append(dg_s)
        du_slots.append(du_s)
        dhn_parts.append(dot(dg_s, w_gate, 1, 0) + dot(du_s, w_up, 1, 0))
    dhn = collect(dhn_parts)
    out_parts = [dot(m_s, w_down, 1, 0) for m_s in m_slots]
    layer_output = (hid + collect(out_parts)).astype(BF)

    order_a, order_b = rep_orders()
    hn_all = jnp.concatenate(hn_slots, 0)
    dy_all = jnp.concatenate(dy_slots, 0)

    def reduced(left_slots, right):
        left = jnp.concatenate(left_slots, 0)
        bit = bit_of(0)
        cols = right.shape[1] // 2
        away = dot(left, lax.dynamic_slice_in_dim(right, (1 - bit) * cols, cols, 1), 0, 0)
        keep = dot(left, lax.dynamic_slice_in_dim(right, bit * cols, cols, 1), 0, 0)
        both = keep + swap(away.astype(BF), 0).astype(F32)
        cut = both.shape[0] // 2
        top = rep_scatter(both[:cut], order_a[1:], 1).astype(BF)
        low = rep_scatter(both[cut:], order_b[1:], 1).astype(BF)
        return jnp.concatenate([rep_gather(top, order_a, 1), rep_gather(low, order_b, 1)], 0)

    d_w_down = reduced(m_slots, dy_all).astype(F32)
    d_w_gate = reduced(dg_slots, hn_all)
    d_w_up = reduced(du_slots, hn_all)
    d_w_in = jnp.stack([d_w_gate, d_w_up], 1).astype(F32)

    d_ffn_gain = jnp.sum(dhn * normed_two, axis=0)
    dhid = dy.astype(F32) + norm_back(dhn, normed_two, inv_two, ffn_gain, 1)
    dab = dhid.astype(BF)

    def reduced_all(x, axis):
        parts = []
        cut = x.shape[2 if axis == 1 else 1] // 2
        for i, order in enumerate((order_a, order_b)):
            piece = x[:, i * cut : (i + 1) * cut] if axis == 2 else x[:, :, i * cut : (i + 1) * cut]
            piece = rep_scatter(piece, order, axis)
            own = collect([lax.dynamic_index_in_dim(piece, s, 0, False) for s in sources])
            parts.append(rep_gather(own.astype(BF), order, axis - 1))
        return jnp.concatenate(parts, 2 - axis).astype(F32)

    members = lax.axis_size("grp")
    d_w_out = reduced_all(dot(ob, dab, 1, 0).reshape(members, w_out.shape[0], width), 2)
    dob = dot(w_out_full, dab, 1, 1).astype(BF)
    dq_rot, dk_part, dv_part = attention_backward(info, q_low, kv, dob, of, soft_inv)
    dq_n = rotate(dq_rot.reshape(QUERY_HEADS, HEAD_SIZE, tokens), cos_t, sin_t, -1.0)
    d_q_gain = jnp.sum(dq_n * q_normed, axis=(0, 2))
    dq = norm_back(dq_n, q_normed, q_inv, q_gain[:, None], 1).reshape(QUERY_WIDTH, tokens)
    dq = dq.astype(BF)
    d_w_q = reduced_all(dot(xn, dq, 0, 1).reshape(members, rows, QUERY_WIDTH), 1)
    dkv_part = jnp.concatenate([dk_part, dv_part], 1)
    dkv = collect([dkv_part[i] for i in range(members)])
    dk_n = rotate(
        dkv[:KEY_VALUE_WIDTH].reshape(KEY_VALUE_HEADS, HEAD_SIZE, tokens), cos_t, sin_t, -1.0
    )
    d_k_gain = jnp.sum(dk_n * k_normed, axis=(0, 2))
    dk = norm_back(dk_n, k_normed, k_inv, k_gain[:, None], 1).reshape(KEY_VALUE_WIDTH, tokens)
    dkv = jnp.concatenate([dk, dkv[KEY_VALUE_WIDTH:]], 0).astype(BF)
    d_w_kv = reduced_all(dot(xn, dkv, 0, 1).reshape(members, rows, 2 * KEY_VALUE_WIDTH), 1)
    d_w_qkv = jnp.concatenate([d_w_q, d_w_kv], 1)

    w_q_full = assemble(w_q, q_shards)
    w_kv_full = assemble(w_kv, kv_shards)
    dxn = dot(dq, w_q_full, 0, 1) + dot(dkv, w_kv_full, 0, 1)
    d_attn_gain = jnp.sum(dxn * normed_one, axis=0)
    input_grad = dhid + norm_back(dxn, normed_one, inv_one, attn_gain, 1)
    gains = sum_everywhere(jnp.concatenate([d_attn_gain, d_ffn_gain, d_q_gain, d_k_gain]))
    return (
        layer_output[None],
        input_grad[None],
        d_w_qkv,
        d_w_out,
        d_w_in,
        d_w_down,
        gains[:width],
        gains[width : 2 * width],
        gains[2 * width : 2 * width + HEAD_SIZE],
        gains[2 * width + HEAD_SIZE :],
    )


def solution(mesh):
    in_specs = (
        P("rep", "grp", None),
        P("grp", None),
        P("grp", None),
        P("grp", None, None),
        P("grp", None),
        P(),
        P(),
        P(),
        P(),
        P("rep", "grp", None),
        P(),
        P("rep"),
    )
    out_specs = (
        P("rep", "grp", None),
        P("rep", "grp", None),
        P("grp", None),
        P("grp", None),
        P("grp", None, None),
        P("grp", None),
        P(),
        P(),
        P(),
        P(),
    )
    return jax.shard_map(
        per_device, mesh=mesh, in_specs=in_specs, out_specs=out_specs, check_vma=False
    )
```

```python
import functools

import jax
import jax.numpy as jnp
from jax import lax
from jax.experimental import pallas as pl
from jax.experimental.pallas import tpu as pltpu
from jax.sharding import PartitionSpec as P

QUERY_HEADS = 20
KEY_VALUE_HEADS = 5
HEAD_SIZE = 64
GROUP = QUERY_HEADS // KEY_VALUE_HEADS
QUERY_WIDTH = QUERY_HEADS * HEAD_SIZE
KEY_VALUE_WIDTH = KEY_VALUE_HEADS * HEAD_SIZE
NORM_EPSILON = 1e-06
ROPE_THETA = 10000.0
LOG2E = 1.4426950408889634
BF = jnp.bfloat16
F32 = jnp.float32


def dot(a, b, ca, cb):
    return lax.dot_general(a, b, (((ca,), (cb,)), ((), ())), preferred_element_type=F32)


def rep_orders():
    bits = lax.axis_size("rep").bit_length() - 1
    rest = list(range(1, bits))
    return [0] + rest, [0] + rest[::-1]


def bit_of(b):
    return (lax.axis_index("rep") >> b) & 1


def swap(x, b):
    n = lax.axis_size("rep")
    return lax.ppermute(x, "rep", [(i, i ^ (1 << b)) for i in range(n)])


def place_of(order):
    place = 0
    for b in order:
        place = place * 2 + bit_of(b)
    return place


def send_half(x, b, axis):
    half = x.shape[axis] // 2
    away = lax.dynamic_slice_in_dim(x, (1 - bit_of(b)) * half, half, axis)
    return swap(away.astype(BF), b)


def add_half(x, recv, b, axis):
    half = x.shape[axis] // 2
    keep = lax.dynamic_slice_in_dim(x, bit_of(b) * half, half, axis)
    return keep.astype(F32) + recv.astype(F32)


def rest_count():
    return lax.axis_size("rep") // 2


def swap_rest(x, j):
    n = lax.axis_size("rep")
    return lax.ppermute(x, "rep", [(i, i ^ (2 * j)) for i in range(n)])


def rest_swaps(x):
    return [x] + [swap_rest(x, j) for j in range(1, rest_count())]


def join_pair(mine, other, b, axis):
    return jnp.where(
        bit_of(b) == 0,
        jnp.concatenate([mine, other], axis),
        jnp.concatenate([other, mine], axis),
    )


def rest_place():
    return lax.axis_index("rep") >> 1


def rest_join(got, axis):
    held = dict(enumerate(got))
    for b in range(rest_count().bit_length() - 1):
        step = 1 << b
        held = {
            i: join_pair(held[i], held[i | step], b + 1, axis) for i in held if not i & step
        }
        held = lax.optimization_barrier(held)
    return held[0]


EDGE = [(0, 1), (1, 0), (2, 3), (3, 2)]
MID = [(1, 2), (2, 1)]
OUTWARD = [(1, 0), (2, 3)]
INWARD = [(0, 1), (3, 2)]


def move(x, pairs):
    return lax.ppermute(x, "grp", pairs)


def ring(n):
    return [(i, (i + 1) % n) for i in range(n)]


class Spread:
    def __init__(self, x):
        self.n = lax.axis_size("grp")
        self.held = [x]

    def hop(self, k):
        held = self.held
        if self.n != 4:
            if k == 1:
                for _ in range(self.n - 1):
                    held.append(move(held[-1], ring(self.n)))
        elif k == 1:
            held += [move(held[0], EDGE), move(held[0], MID)]
        elif k == 2:
            held += [move(held[1], MID), move(held[2], OUTWARD)]
        else:
            held += [move(held[3], OUTWARD)]

    def slot(self, k):
        held = self.held
        if self.n != 4 or k < 2:
            return held[k]
        g = lax.axis_index("grp")
        middle = (g == 1) | (g == 2)
        return jnp.where(middle, held[k], held[k + 2])


class Collect:
    def __init__(self, parts):
        self.n = lax.axis_size("grp")
        self.parts = list(parts)
        self.held = {}

    def send(self, x, pairs):
        return move(x.astype(BF), pairs)

    def plus(self, k, name):
        return self.parts[k].astype(F32) + self.held[name].astype(F32)

    def hop(self, name):
        if self.n != 4:
            return
        parts, held = self.parts, self.held
        if name == "far":
            held["far"] = self.send(parts[3], INWARD)
        elif name == "next":
            held["next"] = self.send(parts[2], INWARD)
        elif name == "far_mid":
            held["far_mid"] = self.send(self.plus(3, "far"), MID)
        elif name == "next_mid":
            held["next_mid"] = self.send(self.plus(2, "next"), MID)
        else:
            held["edge"] = self.send(self.plus(1, "far_mid"), EDGE)

    def result(self):
        parts, held = self.parts, self.held
        if self.n == 4:
            return self.plus(0, "edge") + held["next_mid"].astype(F32)
        total = parts[1].astype(F32)
        for k in list(range(2, self.n)) + [0]:
            total = self.send(total, ring(self.n)).astype(F32) + parts[k].astype(F32)
        return total


def shift(x, k):
    n = lax.axis_size("grp")
    return move(x, [(i, (i + k) % n) for i in range(n)])


def from_shift(k):
    n = lax.axis_size("grp")
    return lax.rem(lax.axis_index("grp") + n - k, n)


class Direct:
    def __init__(self, send):
        n = lax.axis_size("grp")
        self.held = [send[0].astype(F32)] + [shift(send[k].astype(BF), n - k) for k in range(1, n)]

    def result(self):
        total = self.held[0]
        for x in self.held[1:]:
            total = total + x.astype(F32)
        return total


class Shards:
    def __init__(self, w):
        self.w = w
        self.held = None

    def fetch(self):
        n = lax.axis_size("grp")
        size = self.w.shape[0] // lax.axis_size("rep")
        place = bit_of(0) * rest_count() + rest_place()
        mine = lax.dynamic_slice_in_dim(self.w, place * size, size, 0)
        self.held = [shift(mine, k) for k in range(1, n)]

    def rest(self):
        self.held = rest_swaps(jnp.stack(self.held))

    def core(self):
        mine = rest_join(self.held, 1)
        self.held = [mine, swap(mine, 0)]

    def whole(self):
        return join_pair(*self.held, 0, 1)

    def shards(self):
        n = lax.axis_size("grp")
        g = lax.axis_index("grp")
        whole = self.whole()
        return [(g, self.w)] + [(from_shift(k), whole[k - 1]) for k in range(1, n)]


def tie(*values):
    return lax.optimization_barrier(values)


def hold(*movers):
    held = lax.optimization_barrier([m.held for m in movers])
    for m, h in zip(movers, held):
        m.held = h


def hold_with(values, *movers):
    values, held = lax.optimization_barrier((values, [m.held for m in movers]))
    for m, h in zip(movers, held):
        m.held = h
    return values


class Reduced:
    def __init__(self, product, axis):
        self.axis = axis
        core = bit_of(0)
        self.held = [product(1 - core).astype(BF), product(core)]

    def core(self):
        away, keep = self.held
        self.held = [keep, swap(away, 0)]

    def block(self, x, place):
        size = x.shape[self.axis] // rest_count()
        return lax.dynamic_slice_in_dim(x, place * size, size, self.axis)

    def rest(self):
        keep, recv = self.held
        x = keep + recv.astype(F32)
        place = rest_place()
        recv = [
            swap_rest(self.block(x, place ^ j).astype(BF), j) for j in range(1, rest_count())
        ]
        self.held = [x] + recv

    def members(self):
        x = self.block(self.held[0], rest_place())
        for recv in self.held[1:]:
            x = x + recv.astype(F32)
        n = lax.axis_size("grp")
        self.held = Direct(
            [lax.dynamic_index_in_dim(x, from_shift(k), 0, False) for k in range(n)]
        ).held

    def back(self):
        total = self.held[0]
        for x in self.held[1:]:
            total = total + x.astype(F32)
        self.held = rest_swaps(total.astype(BF))

    def last(self):
        mine = rest_join(self.held, self.axis - 1)
        self.held = [mine, swap(mine, 0)]

    def result(self):
        return join_pair(*self.held, 0, self.axis - 1).astype(F32)


class RepSum:
    def __init__(self, away, keep, axis):
        self.axis = axis
        self.held = [away, keep]

    def core(self):
        away, keep = self.held
        self.held = [keep, swap(away, 0)]

    def block(self, x, place):
        size = x.shape[self.axis] // rest_count()
        return lax.dynamic_slice_in_dim(x, place * size, size, self.axis)

    def rest(self):
        keep, recv = self.held
        x = keep + recv.astype(F32)
        place = rest_place()
        recv = [
            swap_rest(self.block(x, place ^ j).astype(BF), j) for j in range(1, rest_count())
        ]
        self.held = [x] + recv

    def back(self):
        x = self.block(self.held[0], rest_place())
        for recv in self.held[1:]:
            x = x + recv.astype(F32)
        self.held = rest_swaps(x.astype(BF))

    def last(self):
        mine = rest_join(self.held, self.axis)
        self.held = [mine, swap(mine, 0)]

    def result(self):
        return join_pair(*self.held, 0, self.axis).astype(F32)


def mask_limit(info_ref, tokens):
    query_pos = info_ref[1] + lax.broadcasted_iota(jnp.int32, (1, tokens), 1)
    return jnp.maximum(query_pos + 1, info_ref[0])


def forward_kernel(info_ref, q_ref, k_ref, v_ref, o_ref, of_ref, inv_ref):
    slots, _, tokens = k_ref.shape
    limit = mask_limit(info_ref, tokens)
    for h in range(GROUP):
        rows = slice(h * HEAD_SIZE, (h + 1) * HEAD_SIZE)
        q = q_ref[rows, :]
        total = jnp.zeros((1, tokens), F32)
        acc = jnp.zeros((HEAD_SIZE, tokens), F32)
        for s in range(slots):
            key_pos = info_ref[2 + s] + lax.broadcasted_iota(jnp.int32, (tokens, tokens), 0)
            t = dot(k_ref[s], q, 0, 0) * (HEAD_SIZE**-0.5 * LOG2E)
            e = jnp.where(key_pos < limit, jnp.exp2(t), 0.0)
            total = total + jnp.sum(e, axis=0, keepdims=True)
            acc = acc + dot(v_ref[s], e.astype(BF), 1, 0)
        inv = 1.0 / total
        out = acc * inv
        o_ref[rows, :] = out.astype(BF)
        of_ref[rows, :] = out
        inv_ref[0, h : h + 1, :] = inv


def backward_kernel(info_ref, q_ref, k_ref, v_ref, g_ref, of_ref, inv_ref, dq_ref, dk_ref, dv_ref):
    slots, _, tokens = k_ref.shape
    limit = mask_limit(info_ref, tokens)
    for h in range(GROUP):
        rows = slice(h * HEAD_SIZE, (h + 1) * HEAD_SIZE)
        q = q_ref[rows, :]
        grad = g_ref[rows, :]
        inv = inv_ref[0, h : h + 1, :]
        delta = jnp.sum(of_ref[rows, :] * grad.astype(F32), axis=0, keepdims=True)
        acc = jnp.zeros((HEAD_SIZE, tokens), F32)
        for s in range(slots):
            key_pos = info_ref[2 + s] + lax.broadcasted_iota(jnp.int32, (tokens, tokens), 0)
            t = dot(k_ref[s], q, 0, 0) * (HEAD_SIZE**-0.5 * LOG2E)
            p = jnp.where(key_pos < limit, jnp.exp2(t) * inv, 0.0)
            dp = dot(v_ref[s], grad, 0, 0)
            ds = (p * (dp - delta)).astype(BF)
            acc = acc + dot(k_ref[s], ds, 1, 0)
            dk = dot(q, ds, 1, 1) * HEAD_SIZE**-0.5
            dv = dot(grad, p.astype(BF), 1, 1)
            if h == 0:
                dk_ref[s] = dk
                dv_ref[s] = dv
            else:
                dk_ref[s] += dk
                dv_ref[s] += dv
        dq_ref[rows, :] = acc * HEAD_SIZE**-0.5


def attention_specs(slots, tokens):
    heads = pl.BlockSpec((GROUP * HEAD_SIZE, tokens), lambda c, info: (c, 0))
    keys = pl.BlockSpec((slots, HEAD_SIZE, tokens), lambda c, info: (0, c, 0))
    values = pl.BlockSpec((slots, HEAD_SIZE, tokens), lambda c, info: (0, KEY_VALUE_HEADS + c, 0))
    inverse = pl.BlockSpec((1, GROUP, tokens), lambda c, info: (c, 0, 0))
    return heads, keys, values, inverse


def attention_forward(info, q, kv):
    slots, _, tokens = kv.shape
    heads, keys, values, inverse = attention_specs(slots, tokens)
    return pl.pallas_call(
        forward_kernel,
        grid_spec=pltpu.PrefetchScalarGridSpec(
            num_scalar_prefetch=1,
            grid=(KEY_VALUE_HEADS,),
            in_specs=[heads, keys, values],
            out_specs=[heads, heads, inverse],
        ),
        out_shape=[
            jax.ShapeDtypeStruct((QUERY_WIDTH, tokens), BF),
            jax.ShapeDtypeStruct((QUERY_WIDTH, tokens), F32),
            jax.ShapeDtypeStruct((KEY_VALUE_HEADS, GROUP, tokens), F32),
        ],
        compiler_params=pltpu.CompilerParams(vmem_limit_bytes=48 * 2**20),
        cost_estimate=pl.CostEstimate(flops=0, bytes_accessed=2**20, transcendentals=0),
        name="attention_forward",
    )(info, q, kv, kv)


def attention_backward(info, q, kv, grad, of, inv):
    slots, _, tokens = kv.shape
    heads, keys, values, inverse = attention_specs(slots, tokens)
    return pl.pallas_call(
        backward_kernel,
        grid_spec=pltpu.PrefetchScalarGridSpec(
            num_scalar_prefetch=1,
            grid=(KEY_VALUE_HEADS,),
            in_specs=[heads, keys, values, heads, heads, inverse],
            out_specs=[heads, keys, keys],
        ),
        out_shape=[
            jax.ShapeDtypeStruct((QUERY_WIDTH, tokens), F32),
            jax.ShapeDtypeStruct((slots, KEY_VALUE_WIDTH, tokens), F32),
            jax.ShapeDtypeStruct((slots, KEY_VALUE_WIDTH, tokens), F32),
        ],
        compiler_params=pltpu.CompilerParams(vmem_limit_bytes=48 * 2**20),
        cost_estimate=pl.CostEstimate(flops=0, bytes_accessed=2**20, transcendentals=0),
        name="attention_backward",
    )(info, q, kv, kv, grad, of, inv)


VMEM = 56 * 2**20


def split_kernel(w_ref, gate_ref, up_ref, s_ref):
    rows = gate_ref.shape[0]
    step = w_ref.shape[0] // rows
    s_ref[...] = w_ref[...].astype(F32)
    for c in range(step // 2):
        lanes = slice(c * 128, (c + 1) * 128)
        gate_ref[:, lanes] = s_ref[pl.ds(2 * c, rows, stride=step), :].astype(BF)
        up_ref[:, lanes] = s_ref[pl.ds(2 * c + 1, rows, stride=step), :].astype(BF)


def split_gate_up(w_in):
    units, _, width = w_in.shape
    step = width // 64
    flat = w_in.reshape(units, 2, width // 128, 128).transpose(0, 2, 1, 3)
    flat = flat.reshape(units * step, 128)
    block = 128
    half = pl.BlockSpec((block, width), lambda i: (i, 0))
    return pl.pallas_call(
        split_kernel,
        grid=(units // block,),
        in_specs=[pl.BlockSpec((block * step, 128), lambda i: (i, 0))],
        out_specs=[half, half],
        out_shape=[jax.ShapeDtypeStruct((units, width), BF)] * 2,
        scratch_shapes=[pltpu.VMEM((block * step, 128), F32)],
        compiler_params=pltpu.CompilerParams(vmem_limit_bytes=VMEM),
        cost_estimate=pl.CostEstimate(flops=0, bytes_accessed=2**20, transcendentals=0),
        name="split_gate_up",
    )(flat)


FFN_CUTS = 5


def ffn_kernel(hn_ref, dy_ref, g_hbm, u_hbm, d_hbm, lhs_ref, dhn_ref, out_ref, wg, wu, wd, sems):
    block = wg.shape[0] // FFN_CUTS
    copies = []
    for i in range(FFN_CUTS):
        rows = pl.ds(i * block, block)
        pairs = ((g_hbm, wg), (u_hbm, wu), (d_hbm, wd))
        copies.append(
            [
                pltpu.make_async_copy(src.at[rows], dst.at[rows], sems.at[j, i])
                for j, (src, dst) in enumerate(pairs)
            ]
        )
        for copy in copies[-1]:
            copy.start()
    hn, dy = hn_ref[...], dy_ref[...]
    for i in range(FFN_CUTS):
        for copy in copies[i]:
            copy.wait()
        rows = pl.ds(i * block, block)
        gate = dot(wg[rows, :], hn, 1, 1)
        up = dot(wu[rows, :], hn, 1, 1)
        dm = dot(wd[rows, :], dy, 1, 1)
        sg = 1.0 / (1.0 + jnp.exp(-gate))
        act = gate * sg
        lhs_ref[0, rows, :] = (act * up).astype(BF)
        lhs_ref[1, rows, :] = (dm * up * sg * (1.0 + gate * (1.0 - sg))).astype(BF)
        lhs_ref[2, rows, :] = (dm * act).astype(BF)
    step = 512
    for n in range(wg.shape[1] // step):
        lanes = pl.ds(n * step, step)
        dhn = dot(lhs_ref[1], wg[:, lanes], 0, 0) + dot(lhs_ref[2], wu[:, lanes], 0, 0)
        dhn_ref[:, lanes] = dhn.astype(dhn_ref.dtype)
        out_ref[:, lanes] = dot(lhs_ref[0], wd[:, lanes], 0, 0).astype(out_ref.dtype)


def ffn_slot(hn, dy, w_gate, w_up, w_down, kind):
    tokens, width = hn.shape
    units = w_gate.shape[0]
    whole = pl.BlockSpec(memory_space=pltpu.VMEM)
    far = pl.BlockSpec(memory_space=pl.ANY)
    return pl.pallas_call(
        ffn_kernel,
        in_specs=[whole, whole, far, far, far],
        out_specs=[whole, whole, whole],
        out_shape=[
            jax.ShapeDtypeStruct((3, units, tokens), BF),
            jax.ShapeDtypeStruct((tokens, width), kind),
            jax.ShapeDtypeStruct((tokens, width), kind),
        ],
        scratch_shapes=[pltpu.VMEM((units, width), BF)] * 3
        + [pltpu.SemaphoreType.DMA((3, FFN_CUTS))],
        compiler_params=pltpu.CompilerParams(vmem_limit_bytes=VMEM),
        cost_estimate=pl.CostEstimate(flops=0, bytes_accessed=2**20, transcendentals=0),
        name="ffn_slot",
    )(hn, dy, w_gate, w_up, w_down)


def grad_kernel(slots, *refs):
    rows = jnp.concatenate([r[0] for r in refs[:slots]], 1)
    right = jnp.concatenate([r[...] for r in refs[slots : 2 * slots]], 0)
    half = right.shape[1] // 2
    out_ref = refs[-1]
    for i in range(2):
        lanes = slice(i * half, (i + 1) * half)
        out_ref[:, lanes] = dot(rows, right[:, lanes], 1, 0).astype(BF)


def weight_grads(c, many, left, right):
    slots = len(left)
    _, units, tokens = left[0].shape
    width = right[0].shape[1]
    cut = units // 2
    lefts = pl.BlockSpec((1, cut, tokens), lambda i, m: (c + i, m, 0))
    rights = pl.BlockSpec((tokens, width), lambda i, m: (0, 0))
    return pl.pallas_call(
        functools.partial(grad_kernel, slots),
        grid=(many, 2),
        in_specs=[lefts] * slots + [rights] * slots,
        out_specs=pl.BlockSpec((cut, width), lambda i, m: (2 * i + m, 0)),
        out_shape=jax.ShapeDtypeStruct((many * units, width), BF),
        compiler_params=pltpu.CompilerParams(vmem_limit_bytes=VMEM),
        cost_estimate=pl.CostEstimate(flops=0, bytes_accessed=2**20, transcendentals=0),
        name="weight_grads",
    )(*left, *right)


def interleave_kernel(gate_ref, up_ref, out_ref):
    out_ref[:, 0, :] = gate_ref[...].astype(F32)
    out_ref[:, 1, :] = up_ref[...].astype(F32)


def interleave(both):
    units, width = both.shape[0] // 2, both.shape[1]
    block = 128
    blocks = units // block
    return pl.pallas_call(
        interleave_kernel,
        grid=(blocks,),
        in_specs=[
            pl.BlockSpec((block, width), lambda i: (i, 0)),
            pl.BlockSpec((block, width), lambda i: (blocks + i, 0)),
        ],
        out_specs=pl.BlockSpec((block, 2, width), lambda i: (i, 0, 0)),
        out_shape=jax.ShapeDtypeStruct((units, 2, width), F32),
        compiler_params=pltpu.CompilerParams(vmem_limit_bytes=VMEM),
        cost_estimate=pl.CostEstimate(flops=0, bytes_accessed=2**20, transcendentals=0),
        name="interleave",
    )(both, both)


def qkv_grad_kernel(slots, info_ref, *refs):
    xn, dq, dkv = refs[:slots], refs[slots : 2 * slots], refs[2 * slots : 3 * slots]
    away_ref, keep_ref = refs[3 * slots :]
    left = jnp.concatenate([r[...] for r in xn], 0)
    split = dq[0].shape[0]
    i = pl.program_id(0)
    for lanes, grads in ((slice(0, split), dq), (slice(split, None), dkv)):
        product = dot(left, jnp.concatenate([r[...] for r in grads], 1), 0, 1)

        @pl.when(i == 0)
        def _():
            away_ref[:, lanes] = product.astype(BF)

        @pl.when(i == 1)
        def _():
            keep_ref[:, lanes] = product


def qkv_grad(core, xn, dq, dkv):
    slots = len(xn)
    tokens, rows = xn[0].shape
    columns = dq[0].shape[0] + dkv[0].shape[0]
    half = pl.BlockSpec((tokens, rows // 2), lambda i, info: (0, info[0] ^ (1 - i)))
    out = pl.BlockSpec((rows // 2, columns), lambda i, info: (0, 0))
    return pl.pallas_call(
        functools.partial(qkv_grad_kernel, slots),
        grid_spec=pltpu.PrefetchScalarGridSpec(
            num_scalar_prefetch=1,
            grid=(2,),
            in_specs=[half] * slots
            + [pl.BlockSpec(x.shape, lambda i, info: (0, 0)) for x in [*dq, *dkv]],
            out_specs=[out, out],
        ),
        out_shape=[
            jax.ShapeDtypeStruct((rows // 2, columns), BF),
            jax.ShapeDtypeStruct((rows // 2, columns), F32),
        ],
        compiler_params=pltpu.CompilerParams(vmem_limit_bytes=VMEM),
        cost_estimate=pl.CostEstimate(flops=0, bytes_accessed=2**20, transcendentals=0),
        name="qkv_grad",
    )(core.reshape(1).astype(jnp.int32), *xn, *dq, *dkv)


def features_kernel(info_ref, dq_ref, dkv_ref, q_ref, kv_ref, more_q_ref, more_kv_ref, out_ref):
    k = pl.program_id(0)

    @pl.when(k == 0)
    def _():
        out_ref[...] = dot(dq_ref[...], q_ref[...], 0, 1) + dot(dkv_ref[...], kv_ref[...], 0, 1)

    @pl.when(k > 0)
    def _():
        product = dot(dq_ref[...], more_q_ref[0], 0, 1)
        out_ref[...] = product + dot(dkv_ref[...], more_kv_ref[0], 0, 1)


def features_grad(sources, dq, dkv, q, kv, more_q, more_kv):
    rows = q.shape[0]
    tokens = dq.shape[1]
    members = len(sources)
    whole = [pl.BlockSpec(x.shape, lambda k, info: (0, 0)) for x in (dq, dkv, q, kv)]
    more = [
        pl.BlockSpec((1,) + x.shape[1:], lambda k, info: (jnp.maximum(k - 1, 0), 0, 0))
        for x in (more_q, more_kv)
    ]
    return pl.pallas_call(
        features_kernel,
        grid_spec=pltpu.PrefetchScalarGridSpec(
            num_scalar_prefetch=1,
            grid=(members,),
            in_specs=whole + more,
            out_specs=pl.BlockSpec((tokens, rows), lambda k, info: (0, info[k])),
        ),
        out_shape=jax.ShapeDtypeStruct((tokens, rows * members), F32),
        compiler_params=pltpu.CompilerParams(vmem_limit_bytes=VMEM),
        cost_estimate=pl.CostEstimate(flops=0, bytes_accessed=2**20, transcendentals=0),
        name="features_grad",
    )(jnp.stack(sources).astype(jnp.int32), dq, dkv, q, kv, more_q, more_kv)


def inverse_rms(values, axis):
    return lax.rsqrt(jnp.mean(values * values, axis=axis, keepdims=True) + NORM_EPSILON)


def norm_back(grad_out, normed, inv_scale, gain, axis):
    scaled = grad_out * gain
    return inv_scale * (scaled - normed * jnp.mean(scaled * normed, axis=axis, keepdims=True))


def rotate(values, cos_t, sin_t, sign):
    half = HEAD_SIZE // 2
    first, second = values[:, :half], values[:, half:]
    sin_t = sin_t * sign
    return jnp.concatenate([first * cos_t - second * sin_t, second * cos_t + first * sin_t], axis=1)


def per_device(
    layer_input,
    w_qkv,
    w_out,
    w_in,
    w_down,
    attn_gain,
    ffn_gain,
    q_gain,
    k_gain,
    cotangent,
    prefix_len,
    seq_slot,
):
    xf = layer_input[0].astype(F32)
    tokens, width = xf.shape
    g = lax.axis_index("grp")
    core = bit_of(0)
    sources = [from_shift(k) for k in range(lax.axis_size("grp"))]
    positions = g * tokens + jnp.arange(tokens, dtype=jnp.int32)
    slot_ids = jnp.arange(prefix_len.shape[0], dtype=jnp.int32)
    prefix = jnp.sum(jnp.where(slot_ids == seq_slot[0], prefix_len, 0))
    info = jnp.stack([prefix, g * tokens] + [s * tokens for s in sources]).astype(jnp.int32)
    half = HEAD_SIZE // 2
    freqs = ROPE_THETA ** (-(2.0 * jnp.arange(half, dtype=F32)) / HEAD_SIZE)
    angles = freqs[:, None] * positions.astype(F32)[None, :]
    cos_t, sin_t = jnp.cos(angles), jnp.sin(angles)
    w_gate, w_up = split_gate_up(w_in)

    inv_one = inverse_rms(xf, 1)
    normed_one = xf * inv_one
    xn = (normed_one * attn_gain).astype(BF)
    dy = cotangent[0]
    rows = w_qkv.shape[0]
    members = lax.axis_size("grp")

    def project(shards):
        total = 0.0
        for source, shard in shards:
            total = total + dot(
                shard, lax.dynamic_slice_in_dim(xn, source * rows, rows, 1), 0, 1
            )
        return total

    kv_w = Shards(w_qkv[:, QUERY_WIDTH:])
    kv_w.fetch()
    xn, w_qkv, w_out, dy, w_in = hold_with((xn, w_qkv, w_out, dy, w_in), kv_w)
    q_w = Shards(w_qkv[:, :QUERY_WIDTH])
    q_w.fetch()
    kv_w.rest()
    w_out, dy, w_in = hold_with((w_out, dy, w_in), kv_w, q_w)
    kv_w.core()
    kv_t = project(kv_w.shards())
    k_raw = kv_t[:KEY_VALUE_WIDTH].reshape(KEY_VALUE_HEADS, HEAD_SIZE, tokens)
    k_inv = inverse_rms(k_raw, 1)
    k_normed = k_raw * k_inv
    k_low = rotate(k_normed * k_gain[:, None], cos_t, sin_t, 1.0).astype(BF)
    local_kv = jnp.concatenate(
        [k_low.reshape(KEY_VALUE_WIDTH, tokens), kv_t[KEY_VALUE_WIDTH:].astype(BF)], 0
    )
    local_kv, dy, w_in, w_out = hold_with((local_kv, dy, w_in, w_out), q_w)
    kv = [local_kv] + [shift(local_kv, k) for k in range(1, members)]
    q_w.rest()
    w_gate, w_up = split_gate_up(w_in)
    kv, w_gate, w_up, dy, w_out = hold_with((kv, w_gate, w_up, dy, w_out), q_w)
    out_w = Shards(w_out)
    out_w.fetch()
    q_w.core()
    q_t = project(q_w.shards())
    q_raw = q_t.reshape(QUERY_HEADS, HEAD_SIZE, tokens)
    q_inv = inverse_rms(q_raw, 1)
    q_normed = q_raw * q_inv
    q_low = rotate(q_normed * q_gain[:, None], cos_t, sin_t, 1.0).astype(BF)
    q_low = q_low.reshape(QUERY_WIDTH, tokens)
    kv, q_low, q_raw, dy = hold_with((kv, q_low, q_raw, dy), out_w)
    kv = jnp.stack(kv)

    dy_s = Spread(dy)
    dy_s.hop(1)
    out_w.rest()
    ob, of, soft_inv = attention_forward(info, q_low, kv)
    ob, of, soft_inv = hold_with((ob, of, soft_inv), out_w, dy_s)
    dy_s.hop(2)
    out_w.core()
    out_shards = out_w.shards()
    hid = xf
    for source, shard in out_shards:
        part = lax.dynamic_slice_in_dim(ob, source * w_out.shape[0], w_out.shape[0], 0)
        hid = hid + dot(part, shard, 0, 0)
    inv_two = inverse_rms(hid, 1)
    normed_two = hid * inv_two
    hn = (normed_two * ffn_gain).astype(BF)
    hn, hid = tie(hn, hid)

    def slot(k):
        kind = F32 if k == 0 else BF
        return ffn_slot(hn_s.slot(k), dy_s.slot(k), w_gate, w_up, w_down, kind)

    hn_s = Spread(hn)
    hn_s.hop(1)
    done = [slot(0)]
    done = hold_with(done, hn_s, dy_s)
    hn_s.hop(2)
    dy_s.hop(3)
    done.append(slot(1))
    done = hold_with(done, hn_s, dy_s)
    hn_s.hop(3)
    done.append(slot(2))
    done = hold_with(done, hn_s)
    dhn_c = Collect([d[1] for d in done])
    dhn_c.parts += [None] * (members - len(dhn_c.parts))
    dhn_c.hop("next")
    done += [slot(k) for k in range(3, members)]
    done = hold_with(done, dhn_c)
    lefts = [d[0] for d in done]
    dhn_c.parts = [d[1] for d in done]
    hn_slots = [hn_s.slot(k) for k in range(members)]
    dy_slots = [dy_s.slot(k) for k in range(members)]
    dhn_c.hop("far")
    dhn_c.hop("next_mid")
    d_down = weight_grads(0, 1, lefts, dy_slots)
    d_in = weight_grads(1, 2, lefts, hn_slots)
    d_down, d_in = hold_with((d_down, d_in), dhn_c)
    d_down = lax.psum(d_down, "rep")
    d_in = lax.psum(d_in, "rep")
    dhn_c.hop("far_mid")
    out_c = Collect([d[2] for d in done])
    out_c.hop("next")
    hold(dhn_c, out_c)
    dhn_c.hop("edge")
    out_c.hop("next_mid")
    hold(dhn_c, out_c)

    dhn = dhn_c.result()
    d_ffn_gain = jnp.sum(dhn * normed_two, axis=0)
    dhid = dy.astype(F32) + norm_back(dhn, normed_two, inv_two, ffn_gain, 1)
    dab = dhid.astype(BF)
    dob = jnp.zeros((QUERY_WIDTH, tokens), BF)
    for source, shard in out_shards:
        part = dot(shard, dab, 1, 1).astype(BF)
        dob = lax.dynamic_update_slice_in_dim(dob, part, source * shard.shape[0], 0)

    def out_grad(i):
        half = lax.dynamic_slice_in_dim(dab, i * (width // 2), width // 2, 1)
        return dot(ob, half, 1, 0).reshape(members, w_out.shape[0], width // 2)

    def columns_of(k):
        member = lax.rem(g + k, members)
        return lax.dynamic_slice_in_dim(xn, member * rows, rows, 1)

    xn_slots = [columns_of(0)] + [shift(columns_of(k), k) for k in range(1, members)]

    w_out_r = Reduced(out_grad, 2)
    dob, xn_slots = hold_with((dob, xn_slots), w_out_r)
    w_out_r.core()
    out_c.hop("far")
    dq_rot, dk_part, dv_part = attention_backward(info, q_low, kv, dob, of, soft_inv)
    dkv_part = [jnp.concatenate([dk_part[k], dv_part[k]], 0) for k in range(members)]
    dkv_part = [dkv_part[0]] + [x.astype(BF) for x in dkv_part[1:]]
    dq_rot, dkv_part = hold_with((dq_rot, dkv_part), w_out_r, out_c)
    dkv_c = Direct(dkv_part)
    dq_n = rotate(dq_rot.reshape(QUERY_HEADS, HEAD_SIZE, tokens), cos_t, sin_t, -1.0)
    d_q_gain = jnp.sum(dq_n * q_normed, axis=(0, 2))
    dq = norm_back(dq_n, q_normed, q_inv, q_gain[:, None], 1).reshape(QUERY_WIDTH, tokens)
    dq = dq.astype(BF)
    dq = hold_with(dq, dkv_c)
    dq_slots = [dq] + [shift(dq, k) for k in range(1, members)]
    w_out_r.rest()
    dkv = dkv_c.result()
    dk_n = rotate(
        dkv[:KEY_VALUE_WIDTH].reshape(KEY_VALUE_HEADS, HEAD_SIZE, tokens), cos_t, sin_t, -1.0
    )
    d_k_gain = jnp.sum(dk_n * k_normed, axis=(0, 2))
    dk = norm_back(dk_n, k_normed, k_inv, k_gain[:, None], 1).reshape(KEY_VALUE_WIDTH, tokens)
    dkv = jnp.concatenate([dk, dkv[KEY_VALUE_WIDTH:]], 0).astype(BF)
    dq_slots, dkv = hold_with((dq_slots, dkv), w_out_r)
    dkv_slots = [dkv] + [shift(dkv, k) for k in range(1, members)]
    w_out_r.members()
    dxn = features_grad(
        sources, dq, dkv, q_w.w, kv_w.w, q_w.whole(), kv_w.whole()
    )
    d_attn_gain = jnp.sum(dxn * normed_one, axis=0)
    input_grad = dhid + norm_back(dxn, normed_one, inv_one, attn_gain, 1)
    gains = jnp.concatenate([d_attn_gain, d_ffn_gain, d_q_gain, d_k_gain])
    dkv_slots, gains, input_grad = hold_with((dkv_slots, gains, input_grad), w_out_r)
    w_out_r.back()
    w_qkv_r = RepSum(*qkv_grad(core, xn_slots, dq_slots, dkv_slots), 0)
    w_qkv_r.core()
    gains = gains + swap(gains, 0)
    gains = hold_with(gains, w_qkv_r, w_out_r)
    w_qkv_r.rest()
    w_out_r.last()
    out_c.hop("far_mid")
    for b in rep_orders()[0][1:]:
        gains = gains + swap(gains, b)
    gains, d_in, d_down = hold_with((gains, d_in, d_down), w_qkv_r, w_out_r, out_c)
    w_qkv_r.back()
    d_w_in = interleave(d_in)
    gains = gains + move(gains, [(i, i ^ 1) for i in range(members)])
    out_c.hop("edge")
    d_w_down = d_down.astype(F32)
    gains, d_w_down, d_w_in = hold_with((gains, d_w_down, d_w_in), w_qkv_r, w_out_r, out_c)
    w_qkv_r.last()
    d_w_out = w_out_r.result()
    for b in range(1, members.bit_length() - 1):
        gains = gains + move(gains, [(i, i ^ (1 << b)) for i in range(members)])
    layer_output = (hid + out_c.result()).astype(BF)
    d_w_out, gains, layer_output = hold_with((d_w_out, gains, layer_output), w_qkv_r)
    d_w_qkv = w_qkv_r.result()
    return (
        layer_output[None],
        input_grad[None],
        d_w_qkv,
        d_w_out,
        d_w_in,
        d_w_down,
        gains[:width],
        gains[width : 2 * width],
        gains[2 * width : 2 * width + HEAD_SIZE],
        gains[2 * width + HEAD_SIZE :],
    )


def solution(mesh):
    in_specs = (
        P("rep", "grp", None),
        P("grp", None),
        P("grp", None),
        P("grp", None, None),
        P("grp", None),
        P(),
        P(),
        P(),
        P(),
        P("rep", "grp", None),
        P(),
        P("rep"),
    )
    out_specs = (
        P("rep", "grp", None),
        P("rep", "grp", None),
        P("grp", None),
        P("grp", None),
        P("grp", None, None),
        P("grp", None),
        P(),
        P(),
        P(),
        P(),
    )
    return jax.shard_map(
        per_device, mesh=mesh, in_specs=in_specs, out_specs=out_specs, check_vma=False
    )
```

```python
import functools

import jax
import jax.numpy as jnp
from jax import lax
from jax.experimental import pallas as pl
from jax.experimental.pallas import tpu as pltpu
from jax.sharding import PartitionSpec as P

QUERY_HEADS = 20
KEY_VALUE_HEADS = 5
HEAD_SIZE = 64
GROUP = QUERY_HEADS // KEY_VALUE_HEADS
QUERY_WIDTH = QUERY_HEADS * HEAD_SIZE
KEY_VALUE_WIDTH = KEY_VALUE_HEADS * HEAD_SIZE
NORM_EPSILON = 1e-06
ROPE_THETA = 10000.0
LOG2E = 1.4426950408889634
BF = jnp.bfloat16
F32 = jnp.float32


def dot(a, b, ca, cb):
    return lax.dot_general(a, b, (((ca,), (cb,)), ((), ())), preferred_element_type=F32)


def rep_orders():
    bits = lax.axis_size("rep").bit_length() - 1
    rest = list(range(1, bits))
    return [0] + rest, [0] + rest[::-1]


def bit_of(b):
    return (lax.axis_index("rep") >> b) & 1


def swap(x, b):
    n = lax.axis_size("rep")
    return lax.ppermute(x, "rep", [(i, i ^ (1 << b)) for i in range(n)])


def place_of(order):
    place = 0
    for b in order:
        place = place * 2 + bit_of(b)
    return place


def send_half(x, b, axis):
    half = x.shape[axis] // 2
    away = lax.dynamic_slice_in_dim(x, (1 - bit_of(b)) * half, half, axis)
    return swap(away.astype(BF), b)


def add_half(x, recv, b, axis):
    half = x.shape[axis] // 2
    keep = lax.dynamic_slice_in_dim(x, bit_of(b) * half, half, axis)
    return keep.astype(F32) + recv.astype(F32)


def rest_count():
    return lax.axis_size("rep") // 2


def swap_rest(x, j):
    n = lax.axis_size("rep")
    return lax.ppermute(x, "rep", [(i, i ^ (2 * j)) for i in range(n)])


def rest_swaps(x):
    return [x] + [swap_rest(x, j) for j in range(1, rest_count())]


def join_pair(mine, other, b, axis):
    return jnp.where(
        bit_of(b) == 0,
        jnp.concatenate([mine, other], axis),
        jnp.concatenate([other, mine], axis),
    )


def rest_place():
    return lax.axis_index("rep") >> 1


def rest_join(got, axis):
    held = dict(enumerate(got))
    for b in range(rest_count().bit_length() - 1):
        step = 1 << b
        held = {
            i: join_pair(held[i], held[i | step], b + 1, axis) for i in held if not i & step
        }
        held = lax.optimization_barrier(held)
    return held[0]


EDGE = [(0, 1), (1, 0), (2, 3), (3, 2)]
MID = [(1, 2), (2, 1)]
OUTWARD = [(1, 0), (2, 3)]
INWARD = [(0, 1), (3, 2)]


def move(x, pairs):
    return lax.ppermute(x, "grp", pairs)


def ring(n):
    return [(i, (i + 1) % n) for i in range(n)]


class Spread:
    def __init__(self, x):
        self.n = lax.axis_size("grp")
        self.held = [x]

    def hop(self, k):
        held = self.held
        if self.n != 4:
            if k == 1:
                for _ in range(self.n - 1):
                    held.append(move(held[-1], ring(self.n)))
        elif k == 1:
            held += [move(held[0], EDGE), move(held[0], MID)]
        elif k == 2:
            held += [move(held[1], MID), move(held[2], OUTWARD)]
        else:
            held += [move(held[3], OUTWARD)]

    def slot(self, k):
        held = self.held
        if self.n != 4 or k < 2:
            return held[k]
        g = lax.axis_index("grp")
        middle = (g == 1) | (g == 2)
        return jnp.where(middle, held[k], held[k + 2])


class Collect:
    def __init__(self, parts):
        self.n = lax.axis_size("grp")
        self.parts = list(parts)
        self.held = {}

    def send(self, x, pairs):
        return move(x.astype(BF), pairs)

    def plus(self, k, name):
        return self.parts[k].astype(F32) + self.held[name].astype(F32)

    def hop(self, name):
        if self.n != 4:
            return
        parts, held = self.parts, self.held
        if name == "far":
            held["far"] = self.send(parts[3], INWARD)
        elif name == "next":
            held["next"] = self.send(parts[2], INWARD)
        elif name == "far_mid":
            held["far_mid"] = self.send(self.plus(3, "far"), MID)
        elif name == "next_mid":
            held["next_mid"] = self.send(self.plus(2, "next"), MID)
        else:
            held["edge"] = self.send(self.plus(1, "far_mid"), EDGE)

    def result(self):
        parts, held = self.parts, self.held
        if self.n == 4:
            return self.plus(0, "edge") + held["next_mid"].astype(F32)
        total = parts[1].astype(F32)
        for k in list(range(2, self.n)) + [0]:
            total = self.send(total, ring(self.n)).astype(F32) + parts[k].astype(F32)
        return total


def shift(x, k):
    n = lax.axis_size("grp")
    return move(x, [(i, (i + k) % n) for i in range(n)])


def from_shift(k):
    n = lax.axis_size("grp")
    return lax.rem(lax.axis_index("grp") + n - k, n)


class Direct:
    def __init__(self, send):
        n = lax.axis_size("grp")
        self.held = [send[0].astype(F32)] + [shift(send[k].astype(BF), n - k) for k in range(1, n)]

    def result(self):
        total = self.held[0]
        for x in self.held[1:]:
            total = total + x.astype(F32)
        return total


class Shards:
    def __init__(self, w):
        self.w = w
        self.held = None

    def fetch(self):
        n = lax.axis_size("grp")
        size = self.w.shape[0] // lax.axis_size("rep")
        place = bit_of(0) * rest_count() + rest_place()
        mine = lax.dynamic_slice_in_dim(self.w, place * size, size, 0)
        self.held = [shift(mine, k) for k in range(1, n)]

    def rest(self):
        self.held = rest_swaps(jnp.stack(self.held))

    def core(self):
        mine = rest_join(self.held, 1)
        self.held = [mine, swap(mine, 0)]

    def whole(self):
        return join_pair(*self.held, 0, 1)

    def shards(self):
        n = lax.axis_size("grp")
        g = lax.axis_index("grp")
        whole = self.whole()
        return [(g, self.w)] + [(from_shift(k), whole[k - 1]) for k in range(1, n)]


def tie(*values):
    return lax.optimization_barrier(values)


def hold(*movers):
    held = lax.optimization_barrier([m.held for m in movers])
    for m, h in zip(movers, held):
        m.held = h


def hold_with(values, *movers):
    values, held = lax.optimization_barrier((values, [m.held for m in movers]))
    for m, h in zip(movers, held):
        m.held = h
    return values


class Reduced:
    def __init__(self, product, axis):
        self.axis = axis
        core = bit_of(0)
        self.held = [product(1 - core).astype(BF), product(core)]

    def core(self):
        away, keep = self.held
        self.held = [keep, swap(away, 0)]

    def block(self, x, place):
        size = x.shape[self.axis] // rest_count()
        return lax.dynamic_slice_in_dim(x, place * size, size, self.axis)

    def rest(self):
        keep, recv = self.held
        x = keep + recv.astype(F32)
        place = rest_place()
        recv = [
            swap_rest(self.block(x, place ^ j).astype(BF), j) for j in range(1, rest_count())
        ]
        self.held = [x] + recv

    def members(self):
        x = self.block(self.held[0], rest_place())
        for recv in self.held[1:]:
            x = x + recv.astype(F32)
        n = lax.axis_size("grp")
        self.held = Direct(
            [lax.dynamic_index_in_dim(x, from_shift(k), 0, False) for k in range(n)]
        ).held

    def back(self):
        total = self.held[0]
        for x in self.held[1:]:
            total = total + x.astype(F32)
        self.held = rest_swaps(total.astype(BF))

    def last(self):
        mine = rest_join(self.held, self.axis - 1)
        self.held = [mine, swap(mine, 0)]

    def result(self):
        return join_pair(*self.held, 0, self.axis - 1).astype(F32)


class RepSum:
    def __init__(self, away, keep, axis):
        self.axis = axis
        self.held = [away, keep]

    def core(self):
        away, keep = self.held
        self.held = [keep, swap(away, 0)]

    def block(self, x, place):
        size = x.shape[self.axis] // rest_count()
        return lax.dynamic_slice_in_dim(x, place * size, size, self.axis)

    def rest(self):
        keep, recv = self.held
        x = keep + recv.astype(F32)
        place = rest_place()
        recv = [
            swap_rest(self.block(x, place ^ j).astype(BF), j) for j in range(1, rest_count())
        ]
        self.held = [x] + recv

    def back(self):
        x = self.block(self.held[0], rest_place())
        for recv in self.held[1:]:
            x = x + recv.astype(F32)
        self.held = rest_swaps(x.astype(BF))

    def last(self):
        mine = rest_join(self.held, self.axis)
        self.held = [mine, swap(mine, 0)]

    def result(self):
        return join_pair(*self.held, 0, self.axis).astype(F32)


def mask_limit(info_ref, tokens):
    query_pos = info_ref[1] + lax.broadcasted_iota(jnp.int32, (1, tokens), 1)
    return jnp.maximum(query_pos + 1, info_ref[0])


def forward_kernel(info_ref, q_ref, k_ref, v_ref, o_ref, of_ref, inv_ref):
    slots, _, tokens = k_ref.shape
    limit = mask_limit(info_ref, tokens)
    for h in range(GROUP):
        rows = slice(h * HEAD_SIZE, (h + 1) * HEAD_SIZE)
        q = q_ref[rows, :]
        total = jnp.zeros((1, tokens), F32)
        acc = jnp.zeros((HEAD_SIZE, tokens), F32)
        for s in range(slots):
            key_pos = info_ref[2 + s] + lax.broadcasted_iota(jnp.int32, (tokens, tokens), 0)
            t = dot(k_ref[s], q, 0, 0) * (HEAD_SIZE**-0.5 * LOG2E)
            e = jnp.where(key_pos < limit, jnp.exp2(t), 0.0)
            total = total + jnp.sum(e, axis=0, keepdims=True)
            acc = acc + dot(v_ref[s], e.astype(BF), 1, 0)
        inv = 1.0 / total
        out = acc * inv
        o_ref[rows, :] = out.astype(BF)
        of_ref[rows, :] = out
        inv_ref[0, h : h + 1, :] = inv


def backward_kernel(info_ref, q_ref, k_ref, v_ref, g_ref, of_ref, inv_ref, dq_ref, dk_ref, dv_ref):
    slots, _, tokens = k_ref.shape
    limit = mask_limit(info_ref, tokens)
    for h in range(GROUP):
        rows = slice(h * HEAD_SIZE, (h + 1) * HEAD_SIZE)
        q = q_ref[rows, :]
        grad = g_ref[rows, :]
        inv = inv_ref[0, h : h + 1, :]
        delta = jnp.sum(of_ref[rows, :] * grad.astype(F32), axis=0, keepdims=True)
        acc = jnp.zeros((HEAD_SIZE, tokens), F32)
        for s in range(slots):
            key_pos = info_ref[2 + s] + lax.broadcasted_iota(jnp.int32, (tokens, tokens), 0)
            t = dot(k_ref[s], q, 0, 0) * (HEAD_SIZE**-0.5 * LOG2E)
            p = jnp.where(key_pos < limit, jnp.exp2(t) * inv, 0.0)
            dp = dot(v_ref[s], grad, 0, 0)
            ds = (p * (dp - delta)).astype(BF)
            acc = acc + dot(k_ref[s], ds, 1, 0)
            dk = dot(q, ds, 1, 1) * HEAD_SIZE**-0.5
            dv = dot(grad, p.astype(BF), 1, 1)
            if h == 0:
                dk_ref[s] = dk
                dv_ref[s] = dv
            else:
                dk_ref[s] += dk
                dv_ref[s] += dv
        dq_ref[rows, :] = acc * HEAD_SIZE**-0.5


def attention_specs(slots, tokens):
    heads = pl.BlockSpec((GROUP * HEAD_SIZE, tokens), lambda c, info: (c, 0))
    keys = pl.BlockSpec((slots, HEAD_SIZE, tokens), lambda c, info: (0, c, 0))
    values = pl.BlockSpec((slots, HEAD_SIZE, tokens), lambda c, info: (0, KEY_VALUE_HEADS + c, 0))
    inverse = pl.BlockSpec((1, GROUP, tokens), lambda c, info: (c, 0, 0))
    return heads, keys, values, inverse


def attention_forward(info, q, kv):
    slots, _, tokens = kv.shape
    heads, keys, values, inverse = attention_specs(slots, tokens)
    return pl.pallas_call(
        forward_kernel,
        grid_spec=pltpu.PrefetchScalarGridSpec(
            num_scalar_prefetch=1,
            grid=(KEY_VALUE_HEADS,),
            in_specs=[heads, keys, values],
            out_specs=[heads, heads, inverse],
        ),
        out_shape=[
            jax.ShapeDtypeStruct((QUERY_WIDTH, tokens), BF),
            jax.ShapeDtypeStruct((QUERY_WIDTH, tokens), F32),
            jax.ShapeDtypeStruct((KEY_VALUE_HEADS, GROUP, tokens), F32),
        ],
        compiler_params=pltpu.CompilerParams(vmem_limit_bytes=48 * 2**20),
        cost_estimate=pl.CostEstimate(flops=0, bytes_accessed=2**20, transcendentals=0),
        name="attention_forward",
    )(info, q, kv, kv)


def attention_backward(info, q, kv, grad, of, inv):
    slots, _, tokens = kv.shape
    heads, keys, values, inverse = attention_specs(slots, tokens)
    return pl.pallas_call(
        backward_kernel,
        grid_spec=pltpu.PrefetchScalarGridSpec(
            num_scalar_prefetch=1,
            grid=(KEY_VALUE_HEADS,),
            in_specs=[heads, keys, values, heads, heads, inverse],
            out_specs=[heads, keys, keys],
        ),
        out_shape=[
            jax.ShapeDtypeStruct((QUERY_WIDTH, tokens), F32),
            jax.ShapeDtypeStruct((slots, KEY_VALUE_WIDTH, tokens), F32),
            jax.ShapeDtypeStruct((slots, KEY_VALUE_WIDTH, tokens), F32),
        ],
        compiler_params=pltpu.CompilerParams(vmem_limit_bytes=48 * 2**20),
        cost_estimate=pl.CostEstimate(flops=0, bytes_accessed=2**20, transcendentals=0),
        name="attention_backward",
    )(info, q, kv, kv, grad, of, inv)


VMEM = 56 * 2**20


def split_kernel(w_ref, gate_ref, up_ref, s_ref):
    rows = gate_ref.shape[0]
    step = w_ref.shape[0] // rows
    s_ref[...] = w_ref[...].astype(F32)
    for c in range(step // 2):
        lanes = slice(c * 128, (c + 1) * 128)
        gate_ref[:, lanes] = s_ref[pl.ds(2 * c, rows, stride=step), :].astype(BF)
        up_ref[:, lanes] = s_ref[pl.ds(2 * c + 1, rows, stride=step), :].astype(BF)


def split_gate_up(w_in):
    units, _, width = w_in.shape
    step = width // 64
    flat = w_in.reshape(units, 2, width // 128, 128).transpose(0, 2, 1, 3)
    flat = flat.reshape(units * step, 128)
    block = 128
    half = pl.BlockSpec((block, width), lambda i: (i, 0))
    return pl.pallas_call(
        split_kernel,
        grid=(units // block,),
        in_specs=[pl.BlockSpec((block * step, 128), lambda i: (i, 0))],
        out_specs=[half, half],
        out_shape=[jax.ShapeDtypeStruct((units, width), BF)] * 2,
        scratch_shapes=[pltpu.VMEM((block * step, 128), F32)],
        compiler_params=pltpu.CompilerParams(vmem_limit_bytes=VMEM),
        cost_estimate=pl.CostEstimate(flops=0, bytes_accessed=2**20, transcendentals=0),
        name="split_gate_up",
    )(flat)


FFN_CUTS = 5


def ffn_kernel(hn_ref, dy_ref, g_hbm, u_hbm, d_hbm, lhs_ref, dhn_ref, out_ref, wg, wu, wd, sems):
    block = wg.shape[0] // FFN_CUTS
    copies = []
    for i in range(FFN_CUTS):
        rows = pl.ds(i * block, block)
        pairs = ((g_hbm, wg), (u_hbm, wu), (d_hbm, wd))
        copies.append(
            [
                pltpu.make_async_copy(src.at[rows], dst.at[rows], sems.at[j, i])
                for j, (src, dst) in enumerate(pairs)
            ]
        )
        for copy in copies[-1]:
            copy.start()
    hn, dy = hn_ref[...], dy_ref[...]
    for i in range(FFN_CUTS):
        for copy in copies[i]:
            copy.wait()
        rows = pl.ds(i * block, block)
        gate = dot(wg[rows, :], hn, 1, 1)
        up = dot(wu[rows, :], hn, 1, 1)
        dm = dot(wd[rows, :], dy, 1, 1)
        sg = 1.0 / (1.0 + jnp.exp(-gate))
        act = gate * sg
        lhs_ref[0, rows, :] = (act * up).astype(BF)
        lhs_ref[1, rows, :] = (dm * up * sg * (1.0 + gate * (1.0 - sg))).astype(BF)
        lhs_ref[2, rows, :] = (dm * act).astype(BF)
    step = 512
    for n in range(wg.shape[1] // step):
        lanes = pl.ds(n * step, step)
        dhn = dot(lhs_ref[1], wg[:, lanes], 0, 0) + dot(lhs_ref[2], wu[:, lanes], 0, 0)
        dhn_ref[:, lanes] = dhn.astype(dhn_ref.dtype)
        out_ref[:, lanes] = dot(lhs_ref[0], wd[:, lanes], 0, 0).astype(out_ref.dtype)


def ffn_slot(hn, dy, w_gate, w_up, w_down, kind):
    tokens, width = hn.shape
    units = w_gate.shape[0]
    whole = pl.BlockSpec(memory_space=pltpu.VMEM)
    far = pl.BlockSpec(memory_space=pl.ANY)
    return pl.pallas_call(
        ffn_kernel,
        in_specs=[whole, whole, far, far, far],
        out_specs=[whole, whole, whole],
        out_shape=[
            jax.ShapeDtypeStruct((3, units, tokens), BF),
            jax.ShapeDtypeStruct((tokens, width), kind),
            jax.ShapeDtypeStruct((tokens, width), kind),
        ],
        scratch_shapes=[pltpu.VMEM((units, width), BF)] * 3
        + [pltpu.SemaphoreType.DMA((3, FFN_CUTS))],
        compiler_params=pltpu.CompilerParams(vmem_limit_bytes=VMEM),
        cost_estimate=pl.CostEstimate(flops=0, bytes_accessed=2**20, transcendentals=0),
        name="ffn_slot",
    )(hn, dy, w_gate, w_up, w_down)


def grad_kernel(slots, *refs):
    left, dy, hn = refs[:slots], refs[slots : 2 * slots], refs[2 * slots : 3 * slots]
    out_ref = refs[-1]
    half = out_ref.shape[1] // 2

    def product(right):
        rows = jnp.concatenate([r[0] for r in left], 1)
        for i in range(2):
            lanes = slice(i * half, (i + 1) * half)
            both = jnp.concatenate([r[:, lanes] for r in right], 0)
            out_ref[:, lanes] = dot(rows, both, 1, 0).astype(BF)

    c = pl.program_id(0)
    pl.when(c == 0)(lambda: product(dy))
    pl.when(c > 0)(lambda: product(hn))


def weight_grads(left, dy, hn):
    slots = len(left)
    _, units, tokens = left[0].shape
    width = dy[0].shape[1]
    cut = units // 2
    lefts = pl.BlockSpec((1, cut, tokens), lambda c, m: (c, m, 0))
    rights = pl.BlockSpec((tokens, width), lambda c, m: (0, 0))
    return pl.pallas_call(
        functools.partial(grad_kernel, slots),
        grid=(3, 2),
        in_specs=[lefts] * slots + [rights] * (2 * slots),
        out_specs=pl.BlockSpec((cut, width), lambda c, m: (2 * c + m, 0)),
        out_shape=jax.ShapeDtypeStruct((3 * units, width), BF),
        compiler_params=pltpu.CompilerParams(vmem_limit_bytes=VMEM),
        cost_estimate=pl.CostEstimate(flops=0, bytes_accessed=2**20, transcendentals=0),
        name="weight_grads",
    )(*left, *dy, *hn)


def widen_kernel(down_ref, gate_ref, up_ref, down_out, in_out):
    down_out[...] = down_ref[...].astype(F32)
    in_out[:, 0, :] = gate_ref[...].astype(F32)
    in_out[:, 1, :] = up_ref[...].astype(F32)


def widen(grads):
    units, width = grads.shape[0] // 3, grads.shape[1]
    block = 128
    blocks = units // block
    return pl.pallas_call(
        widen_kernel,
        grid=(blocks,),
        in_specs=[
            pl.BlockSpec((block, width), lambda i, c=c: (c * blocks + i, 0)) for c in range(3)
        ],
        out_specs=[
            pl.BlockSpec((block, width), lambda i: (i, 0)),
            pl.BlockSpec((block, 2, width), lambda i: (i, 0, 0)),
        ],
        out_shape=[
            jax.ShapeDtypeStruct((units, width), F32),
            jax.ShapeDtypeStruct((units, 2, width), F32),
        ],
        compiler_params=pltpu.CompilerParams(vmem_limit_bytes=VMEM),
        cost_estimate=pl.CostEstimate(flops=0, bytes_accessed=2**20, transcendentals=0),
        name="widen",
    )(grads, grads, grads)


def qkv_grad_kernel(slots, info_ref, *refs):
    xn, dq, dkv = refs[:slots], refs[slots : 2 * slots], refs[2 * slots : 3 * slots]
    away_ref, keep_ref = refs[3 * slots :]
    left = jnp.concatenate([r[...] for r in xn], 0)
    split = dq[0].shape[0]
    i = pl.program_id(0)
    for lanes, grads in ((slice(0, split), dq), (slice(split, None), dkv)):
        product = dot(left, jnp.concatenate([r[...] for r in grads], 1), 0, 1)

        @pl.when(i == 0)
        def _():
            away_ref[:, lanes] = product.astype(BF)

        @pl.when(i == 1)
        def _():
            keep_ref[:, lanes] = product


def qkv_grad(core, xn, dq, dkv):
    slots = len(xn)
    tokens, rows = xn[0].shape
    columns = dq[0].shape[0] + dkv[0].shape[0]
    half = pl.BlockSpec((tokens, rows // 2), lambda i, info: (0, info[0] ^ (1 - i)))
    out = pl.BlockSpec((rows // 2, columns), lambda i, info: (0, 0))
    return pl.pallas_call(
        functools.partial(qkv_grad_kernel, slots),
        grid_spec=pltpu.PrefetchScalarGridSpec(
            num_scalar_prefetch=1,
            grid=(2,),
            in_specs=[half] * slots
            + [pl.BlockSpec(x.shape, lambda i, info: (0, 0)) for x in [*dq, *dkv]],
            out_specs=[out, out],
        ),
        out_shape=[
            jax.ShapeDtypeStruct((rows // 2, columns), BF),
            jax.ShapeDtypeStruct((rows // 2, columns), F32),
        ],
        compiler_params=pltpu.CompilerParams(vmem_limit_bytes=VMEM),
        cost_estimate=pl.CostEstimate(flops=0, bytes_accessed=2**20, transcendentals=0),
        name="qkv_grad",
    )(core.reshape(1).astype(jnp.int32), *xn, *dq, *dkv)


def features_kernel(info_ref, dq_ref, dkv_ref, q_ref, kv_ref, more_q_ref, more_kv_ref, out_ref):
    k = pl.program_id(0)

    @pl.when(k == 0)
    def _():
        out_ref[...] = dot(dq_ref[...], q_ref[...], 0, 1) + dot(dkv_ref[...], kv_ref[...], 0, 1)

    @pl.when(k > 0)
    def _():
        product = dot(dq_ref[...], more_q_ref[0], 0, 1)
        out_ref[...] = product + dot(dkv_ref[...], more_kv_ref[0], 0, 1)


def features_grad(sources, dq, dkv, q, kv, more_q, more_kv):
    rows = q.shape[0]
    tokens = dq.shape[1]
    members = len(sources)
    whole = [pl.BlockSpec(x.shape, lambda k, info: (0, 0)) for x in (dq, dkv, q, kv)]
    more = [
        pl.BlockSpec((1,) + x.shape[1:], lambda k, info: (jnp.maximum(k - 1, 0), 0, 0))
        for x in (more_q, more_kv)
    ]
    return pl.pallas_call(
        features_kernel,
        grid_spec=pltpu.PrefetchScalarGridSpec(
            num_scalar_prefetch=1,
            grid=(members,),
            in_specs=whole + more,
            out_specs=pl.BlockSpec((tokens, rows), lambda k, info: (0, info[k])),
        ),
        out_shape=jax.ShapeDtypeStruct((tokens, rows * members), F32),
        compiler_params=pltpu.CompilerParams(vmem_limit_bytes=VMEM),
        cost_estimate=pl.CostEstimate(flops=0, bytes_accessed=2**20, transcendentals=0),
        name="features_grad",
    )(jnp.stack(sources).astype(jnp.int32), dq, dkv, q, kv, more_q, more_kv)


def inverse_rms(values, axis):
    return lax.rsqrt(jnp.mean(values * values, axis=axis, keepdims=True) + NORM_EPSILON)


def norm_back(grad_out, normed, inv_scale, gain, axis):
    scaled = grad_out * gain
    return inv_scale * (scaled - normed * jnp.mean(scaled * normed, axis=axis, keepdims=True))


def rotate(values, cos_t, sin_t, sign):
    half = HEAD_SIZE // 2
    first, second = values[:, :half], values[:, half:]
    sin_t = sin_t * sign
    return jnp.concatenate([first * cos_t - second * sin_t, second * cos_t + first * sin_t], axis=1)


def per_device(
    layer_input,
    w_qkv,
    w_out,
    w_in,
    w_down,
    attn_gain,
    ffn_gain,
    q_gain,
    k_gain,
    cotangent,
    prefix_len,
    seq_slot,
):
    xf = layer_input[0].astype(F32)
    tokens, width = xf.shape
    g = lax.axis_index("grp")
    core = bit_of(0)
    sources = [from_shift(k) for k in range(lax.axis_size("grp"))]
    positions = g * tokens + jnp.arange(tokens, dtype=jnp.int32)
    slot_ids = jnp.arange(prefix_len.shape[0], dtype=jnp.int32)
    prefix = jnp.sum(jnp.where(slot_ids == seq_slot[0], prefix_len, 0))
    info = jnp.stack([prefix, g * tokens] + [s * tokens for s in sources]).astype(jnp.int32)
    half = HEAD_SIZE // 2
    freqs = ROPE_THETA ** (-(2.0 * jnp.arange(half, dtype=F32)) / HEAD_SIZE)
    angles = freqs[:, None] * positions.astype(F32)[None, :]
    cos_t, sin_t = jnp.cos(angles), jnp.sin(angles)
    w_gate, w_up = split_gate_up(w_in)

    inv_one = inverse_rms(xf, 1)
    normed_one = xf * inv_one
    xn = (normed_one * attn_gain).astype(BF)
    dy = cotangent[0]
    rows = w_qkv.shape[0]
    members = lax.axis_size("grp")

    def project(shards):
        total = 0.0
        for source, shard in shards:
            total = total + dot(
                shard, lax.dynamic_slice_in_dim(xn, source * rows, rows, 1), 0, 1
            )
        return total

    kv_w = Shards(w_qkv[:, QUERY_WIDTH:])
    kv_w.fetch()
    xn, w_qkv, w_out, dy, w_in = hold_with((xn, w_qkv, w_out, dy, w_in), kv_w)
    q_w = Shards(w_qkv[:, :QUERY_WIDTH])
    q_w.fetch()
    kv_w.rest()
    w_out, dy, w_in = hold_with((w_out, dy, w_in), kv_w, q_w)
    kv_w.core()
    kv_t = project(kv_w.shards())
    k_raw = kv_t[:KEY_VALUE_WIDTH].reshape(KEY_VALUE_HEADS, HEAD_SIZE, tokens)
    k_inv = inverse_rms(k_raw, 1)
    k_normed = k_raw * k_inv
    k_low = rotate(k_normed * k_gain[:, None], cos_t, sin_t, 1.0).astype(BF)
    local_kv = jnp.concatenate(
        [k_low.reshape(KEY_VALUE_WIDTH, tokens), kv_t[KEY_VALUE_WIDTH:].astype(BF)], 0
    )
    local_kv, dy, w_in, w_out = hold_with((local_kv, dy, w_in, w_out), q_w)
    kv = [local_kv] + [shift(local_kv, k) for k in range(1, members)]
    q_w.rest()
    w_gate, w_up = split_gate_up(w_in)
    kv, w_gate, w_up, dy, w_out = hold_with((kv, w_gate, w_up, dy, w_out), q_w)
    out_w = Shards(w_out)
    out_w.fetch()
    q_w.core()
    q_t = project(q_w.shards())
    q_raw = q_t.reshape(QUERY_HEADS, HEAD_SIZE, tokens)
    q_inv = inverse_rms(q_raw, 1)
    q_normed = q_raw * q_inv
    q_low = rotate(q_normed * q_gain[:, None], cos_t, sin_t, 1.0).astype(BF)
    q_low = q_low.reshape(QUERY_WIDTH, tokens)
    dy_s = Spread(dy)
    dy_s.hop(1)
    kv, q_low, q_raw = hold_with((kv, q_low, q_raw), out_w, dy_s)
    kv = jnp.stack(kv)

    dy_s.hop(2)
    out_w.rest()
    ob, of, soft_inv = attention_forward(info, q_low, kv)
    ob, of, soft_inv = hold_with((ob, of, soft_inv), out_w, dy_s)
    dy_s.hop(3)
    out_w.core()
    out_shards = out_w.shards()
    hid = xf
    for source, shard in out_shards:
        part = lax.dynamic_slice_in_dim(ob, source * w_out.shape[0], w_out.shape[0], 0)
        hid = hid + dot(part, shard, 0, 0)
    inv_two = inverse_rms(hid, 1)
    normed_two = hid * inv_two
    hn = (normed_two * ffn_gain).astype(BF)
    hn, hid = tie(hn, hid)

    def slot(k):
        kind = F32 if k == 0 else BF
        return ffn_slot(hn_s.slot(k), dy_s.slot(k), w_gate, w_up, w_down, kind)

    hn_s = Spread(hn)
    hn_s.hop(1)
    done = [slot(0)]
    done = hold_with(done, hn_s, dy_s)
    hn_s.hop(2)
    done.append(slot(1))
    done = hold_with(done, hn_s, dy_s)
    hn_s.hop(3)
    done.append(slot(2))
    done = hold_with(done, hn_s)
    dhn_c = Collect([d[1] for d in done])
    dhn_c.parts += [None] * (members - len(dhn_c.parts))
    dhn_c.hop("next")
    done += [slot(k) for k in range(3, members)]
    done = hold_with(done, dhn_c)
    lefts = [d[0] for d in done]
    dhn_c.parts = [d[1] for d in done]
    hn_slots = [hn_s.slot(k) for k in range(members)]
    dy_slots = [dy_s.slot(k) for k in range(members)]
    dhn_c.hop("far")
    dhn_c.hop("next_mid")
    grads = weight_grads(lefts, dy_slots, hn_slots)
    grads = hold_with(grads, dhn_c)
    grads = lax.psum_scatter(grads, "rep", scatter_dimension=0, tiled=True)
    dhn_c.hop("far_mid")
    out_c = Collect([d[2] for d in done])
    out_c.hop("next")
    hold(dhn_c, out_c)
    dhn_c.hop("edge")
    out_c.hop("next_mid")
    hold(dhn_c, out_c)

    dhn = dhn_c.result()
    d_ffn_gain = jnp.sum(dhn * normed_two, axis=0)
    dhid = dy.astype(F32) + norm_back(dhn, normed_two, inv_two, ffn_gain, 1)
    dab = dhid.astype(BF)
    dob = jnp.zeros((QUERY_WIDTH, tokens), BF)
    for source, shard in out_shards:
        part = dot(shard, dab, 1, 1).astype(BF)
        dob = lax.dynamic_update_slice_in_dim(dob, part, source * shard.shape[0], 0)

    def out_grad(i):
        half = lax.dynamic_slice_in_dim(dab, i * (width // 2), width // 2, 1)
        return dot(ob, half, 1, 0).reshape(members, w_out.shape[0], width // 2)

    def columns_of(k):
        member = lax.rem(g + k, members)
        return lax.dynamic_slice_in_dim(xn, member * rows, rows, 1)

    xn_slots = [columns_of(0)] + [shift(columns_of(k), k) for k in range(1, members)]

    w_out_r = Reduced(out_grad, 2)
    dob, xn_slots = hold_with((dob, xn_slots), w_out_r)
    w_out_r.core()
    out_c.hop("far")
    dq_rot, dk_part, dv_part = attention_backward(info, q_low, kv, dob, of, soft_inv)
    dkv_part = [jnp.concatenate([dk_part[k], dv_part[k]], 0) for k in range(members)]
    dkv_part = [dkv_part[0]] + [x.astype(BF) for x in dkv_part[1:]]
    dq_rot, dkv_part = hold_with((dq_rot, dkv_part), w_out_r, out_c)
    dkv_c = Direct(dkv_part)
    dq_n = rotate(dq_rot.reshape(QUERY_HEADS, HEAD_SIZE, tokens), cos_t, sin_t, -1.0)
    d_q_gain = jnp.sum(dq_n * q_normed, axis=(0, 2))
    dq = norm_back(dq_n, q_normed, q_inv, q_gain[:, None], 1).reshape(QUERY_WIDTH, tokens)
    dq = dq.astype(BF)
    dq, grads = hold_with((dq, grads), dkv_c)
    grads = lax.all_gather(grads, "rep", axis=0, tiled=True)
    dq_slots = [dq] + [shift(dq, k) for k in range(1, members)]
    w_out_r.rest()
    dkv = dkv_c.result()
    dk_n = rotate(
        dkv[:KEY_VALUE_WIDTH].reshape(KEY_VALUE_HEADS, HEAD_SIZE, tokens), cos_t, sin_t, -1.0
    )
    d_k_gain = jnp.sum(dk_n * k_normed, axis=(0, 2))
    dk = norm_back(dk_n, k_normed, k_inv, k_gain[:, None], 1).reshape(KEY_VALUE_WIDTH, tokens)
    dkv = jnp.concatenate([dk, dkv[KEY_VALUE_WIDTH:]], 0).astype(BF)
    dq_slots, dkv = hold_with((dq_slots, dkv), w_out_r)
    dkv_slots = [dkv] + [shift(dkv, k) for k in range(1, members)]
    w_out_r.members()
    dxn = features_grad(
        sources, dq, dkv, q_w.w, kv_w.w, q_w.whole(), kv_w.whole()
    )
    d_attn_gain = jnp.sum(dxn * normed_one, axis=0)
    input_grad = dhid + norm_back(dxn, normed_one, inv_one, attn_gain, 1)
    gains = jnp.concatenate([d_attn_gain, d_ffn_gain, d_q_gain, d_k_gain])
    dkv_slots, gains, input_grad = hold_with((dkv_slots, gains, input_grad), w_out_r)
    w_out_r.back()
    w_qkv_r = RepSum(*qkv_grad(core, xn_slots, dq_slots, dkv_slots), 0)
    w_qkv_r.core()
    gains = gains + swap(gains, 0)
    gains = hold_with(gains, w_qkv_r, w_out_r)
    w_qkv_r.rest()
    w_out_r.last()
    out_c.hop("far_mid")
    for b in rep_orders()[0][1:]:
        gains = gains + swap(gains, b)
    gains, grads = hold_with((gains, grads), w_qkv_r, w_out_r, out_c)
    w_qkv_r.back()
    d_w_down, d_w_in = widen(grads)
    gains = gains + move(gains, [(i, i ^ 1) for i in range(members)])
    out_c.hop("edge")
    gains, d_w_down, d_w_in = hold_with((gains, d_w_down, d_w_in), w_qkv_r, w_out_r, out_c)
    w_qkv_r.last()
    d_w_out = w_out_r.result()
    for b in range(1, members.bit_length() - 1):
        gains = gains + move(gains, [(i, i ^ (1 << b)) for i in range(members)])
    layer_output = (hid + out_c.result()).astype(BF)
    d_w_out, gains, layer_output = hold_with((d_w_out, gains, layer_output), w_qkv_r)
    d_w_qkv = w_qkv_r.result()
    return (
        layer_output[None],
        input_grad[None],
        d_w_qkv,
        d_w_out,
        d_w_in,
        d_w_down,
        gains[:width],
        gains[width : 2 * width],
        gains[2 * width : 2 * width + HEAD_SIZE],
        gains[2 * width + HEAD_SIZE :],
    )


def solution(mesh):
    in_specs = (
        P("rep", "grp", None),
        P("grp", None),
        P("grp", None),
        P("grp", None, None),
        P("grp", None),
        P(),
        P(),
        P(),
        P(),
        P("rep", "grp", None),
        P(),
        P("rep"),
    )
    out_specs = (
        P("rep", "grp", None),
        P("rep", "grp", None),
        P("grp", None),
        P("grp", None),
        P("grp", None, None),
        P("grp", None),
        P(),
        P(),
        P(),
        P(),
    )
    return jax.shard_map(
        per_device, mesh=mesh, in_specs=in_specs, out_specs=out_specs, check_vma=False
    )
```

```python
import functools

import jax
import jax.numpy as jnp
from jax import lax
from jax.experimental import pallas as pl
from jax.experimental.pallas import tpu as pltpu
from jax.sharding import PartitionSpec as P

QUERY_HEADS = 20
KEY_VALUE_HEADS = 5
HEAD_SIZE = 64
GROUP = QUERY_HEADS // KEY_VALUE_HEADS
QUERY_WIDTH = QUERY_HEADS * HEAD_SIZE
KEY_VALUE_WIDTH = KEY_VALUE_HEADS * HEAD_SIZE
NORM_EPSILON = 1e-06
ROPE_THETA = 10000.0
LOG2E = 1.4426950408889634
BF = jnp.bfloat16
F32 = jnp.float32


def dot(a, b, ca, cb):
    return lax.dot_general(a, b, (((ca,), (cb,)), ((), ())), preferred_element_type=F32)


def rep_orders():
    bits = lax.axis_size("rep").bit_length() - 1
    rest = list(range(1, bits))
    return [0] + rest, [0] + rest[::-1]


def bit_of(b):
    return (lax.axis_index("rep") >> b) & 1


def swap(x, b):
    n = lax.axis_size("rep")
    return lax.ppermute(x, "rep", [(i, i ^ (1 << b)) for i in range(n)])


def place_of(order):
    place = 0
    for b in order:
        place = place * 2 + bit_of(b)
    return place


def send_half(x, b, axis):
    half = x.shape[axis] // 2
    away = lax.dynamic_slice_in_dim(x, (1 - bit_of(b)) * half, half, axis)
    return swap(away.astype(BF), b)


def add_half(x, recv, b, axis):
    half = x.shape[axis] // 2
    keep = lax.dynamic_slice_in_dim(x, bit_of(b) * half, half, axis)
    return keep.astype(F32) + recv.astype(F32)


def rest_count():
    return lax.axis_size("rep") // 2


def swap_rest(x, j):
    n = lax.axis_size("rep")
    return lax.ppermute(x, "rep", [(i, i ^ (2 * j)) for i in range(n)])


def rest_swaps(x):
    return [x] + [swap_rest(x, j) for j in range(1, rest_count())]


def join_pair(mine, other, b, axis):
    return jnp.where(
        bit_of(b) == 0,
        jnp.concatenate([mine, other], axis),
        jnp.concatenate([other, mine], axis),
    )


def rest_place():
    return lax.axis_index("rep") >> 1


def rest_join(got, axis):
    held = dict(enumerate(got))
    for b in range(rest_count().bit_length() - 1):
        step = 1 << b
        held = {
            i: join_pair(held[i], held[i | step], b + 1, axis) for i in held if not i & step
        }
        held = lax.optimization_barrier(held)
    return held[0]


EDGE = [(0, 1), (1, 0), (2, 3), (3, 2)]
MID = [(1, 2), (2, 1)]
OUTWARD = [(1, 0), (2, 3)]
INWARD = [(0, 1), (3, 2)]


def move(x, pairs):
    return lax.ppermute(x, "grp", pairs)


def ring(n):
    return [(i, (i + 1) % n) for i in range(n)]


class Spread:
    def __init__(self, x):
        self.n = lax.axis_size("grp")
        self.held = [x]

    def hop(self, k):
        held = self.held
        if self.n != 4:
            if k == 1:
                for _ in range(self.n - 1):
                    held.append(move(held[-1], ring(self.n)))
        elif k == 1:
            held += [move(held[0], EDGE), move(held[0], MID)]
        elif k == 2:
            held += [move(held[1], MID), move(held[2], OUTWARD)]
        else:
            held += [move(held[3], OUTWARD)]

    def slot(self, k):
        held = self.held
        if self.n != 4 or k < 2:
            return held[k]
        g = lax.axis_index("grp")
        middle = (g == 1) | (g == 2)
        return jnp.where(middle, held[k], held[k + 2])


class Collect:
    def __init__(self, parts):
        self.n = lax.axis_size("grp")
        self.parts = list(parts)
        self.held = {}

    def send(self, x, pairs):
        return move(x.astype(BF), pairs)

    def plus(self, k, name):
        return self.parts[k].astype(F32) + self.held[name].astype(F32)

    def hop(self, name):
        if self.n != 4:
            return
        parts, held = self.parts, self.held
        if name == "far":
            held["far"] = self.send(parts[3], INWARD)
        elif name == "next":
            held["next"] = self.send(parts[2], INWARD)
        elif name == "far_mid":
            held["far_mid"] = self.send(self.plus(3, "far"), MID)
        elif name == "next_mid":
            held["next_mid"] = self.send(self.plus(2, "next"), MID)
        else:
            held["edge"] = self.send(self.plus(1, "far_mid"), EDGE)

    def result(self):
        parts, held = self.parts, self.held
        if self.n == 4:
            return self.plus(0, "edge") + held["next_mid"].astype(F32)
        total = parts[1].astype(F32)
        for k in list(range(2, self.n)) + [0]:
            total = self.send(total, ring(self.n)).astype(F32) + parts[k].astype(F32)
        return total


def shift(x, k):
    n = lax.axis_size("grp")
    return move(x, [(i, (i + k) % n) for i in range(n)])


def from_shift(k):
    n = lax.axis_size("grp")
    return lax.rem(lax.axis_index("grp") + n - k, n)


class Direct:
    def __init__(self, send):
        n = lax.axis_size("grp")
        self.held = [send[0].astype(F32)] + [shift(send[k].astype(BF), n - k) for k in range(1, n)]

    def result(self):
        total = self.held[0]
        for x in self.held[1:]:
            total = total + x.astype(F32)
        return total


class Shards:
    def __init__(self, w):
        self.w = w
        self.held = None

    def fetch(self):
        n = lax.axis_size("grp")
        size = self.w.shape[0] // lax.axis_size("rep")
        place = bit_of(0) * rest_count() + rest_place()
        mine = lax.dynamic_slice_in_dim(self.w, place * size, size, 0)
        self.held = [shift(mine, k) for k in range(1, n)]

    def rest(self):
        self.held = rest_swaps(jnp.stack(self.held))

    def core(self):
        mine = rest_join(self.held, 1)
        self.held = [mine, swap(mine, 0)]

    def whole(self):
        return join_pair(*self.held, 0, 1)

    def shards(self):
        n = lax.axis_size("grp")
        g = lax.axis_index("grp")
        whole = self.whole()
        return [(g, self.w)] + [(from_shift(k), whole[k - 1]) for k in range(1, n)]


def tie(*values):
    return lax.optimization_barrier(values)


def hold(*movers):
    held = lax.optimization_barrier([m.held for m in movers])
    for m, h in zip(movers, held):
        m.held = h


def hold_with(values, *movers):
    values, held = lax.optimization_barrier((values, [m.held for m in movers]))
    for m, h in zip(movers, held):
        m.held = h
    return values


class Reduced:
    def __init__(self, product, axis):
        self.axis = axis
        core = bit_of(0)
        self.held = [product(1 - core).astype(BF), product(core)]

    def core(self):
        away, keep = self.held
        self.held = [keep, swap(away, 0)]

    def block(self, x, place):
        size = x.shape[self.axis] // rest_count()
        return lax.dynamic_slice_in_dim(x, place * size, size, self.axis)

    def rest(self):
        keep, recv = self.held
        x = keep + recv.astype(F32)
        place = rest_place()
        recv = [
            swap_rest(self.block(x, place ^ j).astype(BF), j) for j in range(1, rest_count())
        ]
        self.held = [x] + recv

    def members(self):
        x = self.block(self.held[0], rest_place())
        for recv in self.held[1:]:
            x = x + recv.astype(F32)
        n = lax.axis_size("grp")
        self.held = Direct(
            [lax.dynamic_index_in_dim(x, from_shift(k), 0, False) for k in range(n)]
        ).held

    def back(self):
        total = self.held[0]
        for x in self.held[1:]:
            total = total + x.astype(F32)
        self.held = rest_swaps(total.astype(BF))

    def last(self):
        mine = rest_join(self.held, self.axis - 1)
        self.held = [mine, swap(mine, 0)]

    def result(self):
        return join_pair(*self.held, 0, self.axis - 1).astype(F32)


class RepSum:
    def __init__(self, away, keep, axis):
        self.axis = axis
        self.held = [away, keep]

    def core(self):
        away, keep = self.held
        self.held = [keep, swap(away, 0)]

    def block(self, x, place):
        size = x.shape[self.axis] // rest_count()
        return lax.dynamic_slice_in_dim(x, place * size, size, self.axis)

    def rest(self):
        keep, recv = self.held
        x = keep + recv.astype(F32)
        place = rest_place()
        recv = [
            swap_rest(self.block(x, place ^ j).astype(BF), j) for j in range(1, rest_count())
        ]
        self.held = [x] + recv

    def back(self):
        x = self.block(self.held[0], rest_place())
        for recv in self.held[1:]:
            x = x + recv.astype(F32)
        self.held = rest_swaps(x.astype(BF))

    def last(self):
        mine = rest_join(self.held, self.axis)
        self.held = [mine, swap(mine, 0)]

    def result(self):
        return join_pair(*self.held, 0, self.axis).astype(F32)


def mask_limit(info_ref, tokens):
    query_pos = info_ref[1] + lax.broadcasted_iota(jnp.int32, (1, tokens), 1)
    return jnp.maximum(query_pos + 1, info_ref[0])


def forward_kernel(info_ref, q_ref, k_ref, v_ref, o_ref, of_ref, inv_ref):
    slots, _, tokens = k_ref.shape
    limit = mask_limit(info_ref, tokens)
    for h in range(GROUP):
        rows = slice(h * HEAD_SIZE, (h + 1) * HEAD_SIZE)
        q = q_ref[rows, :]
        total = jnp.zeros((1, tokens), F32)
        acc = jnp.zeros((HEAD_SIZE, tokens), F32)
        for s in range(slots):
            key_pos = info_ref[2 + s] + lax.broadcasted_iota(jnp.int32, (tokens, tokens), 0)
            t = dot(k_ref[s], q, 0, 0) * (HEAD_SIZE**-0.5 * LOG2E)
            e = jnp.where(key_pos < limit, jnp.exp2(t), 0.0)
            total = total + jnp.sum(e, axis=0, keepdims=True)
            acc = acc + dot(v_ref[s], e.astype(BF), 1, 0)
        inv = 1.0 / total
        out = acc * inv
        o_ref[rows, :] = out.astype(BF)
        of_ref[rows, :] = out
        inv_ref[0, h : h + 1, :] = inv


def backward_kernel(info_ref, q_ref, k_ref, v_ref, g_ref, of_ref, inv_ref, dq_ref, dk_ref, dv_ref):
    slots, _, tokens = k_ref.shape
    limit = mask_limit(info_ref, tokens)
    for h in range(GROUP):
        rows = slice(h * HEAD_SIZE, (h + 1) * HEAD_SIZE)
        q = q_ref[rows, :]
        grad = g_ref[rows, :]
        inv = inv_ref[0, h : h + 1, :]
        delta = jnp.sum(of_ref[rows, :] * grad.astype(F32), axis=0, keepdims=True)
        acc = jnp.zeros((HEAD_SIZE, tokens), F32)
        for s in range(slots):
            key_pos = info_ref[2 + s] + lax.broadcasted_iota(jnp.int32, (tokens, tokens), 0)
            t = dot(k_ref[s], q, 0, 0) * (HEAD_SIZE**-0.5 * LOG2E)
            p = jnp.where(key_pos < limit, jnp.exp2(t) * inv, 0.0)
            dp = dot(v_ref[s], grad, 0, 0)
            ds = (p * (dp - delta)).astype(BF)
            acc = acc + dot(k_ref[s], ds, 1, 0)
            dk = dot(q, ds, 1, 1) * HEAD_SIZE**-0.5
            dv = dot(grad, p.astype(BF), 1, 1)
            if h == 0:
                dk_ref[s] = dk
                dv_ref[s] = dv
            else:
                dk_ref[s] += dk
                dv_ref[s] += dv
        dq_ref[rows, :] = acc * HEAD_SIZE**-0.5


def attention_specs(slots, tokens):
    heads = pl.BlockSpec((GROUP * HEAD_SIZE, tokens), lambda c, info: (c, 0))
    keys = pl.BlockSpec((slots, HEAD_SIZE, tokens), lambda c, info: (0, c, 0))
    values = pl.BlockSpec((slots, HEAD_SIZE, tokens), lambda c, info: (0, KEY_VALUE_HEADS + c, 0))
    inverse = pl.BlockSpec((1, GROUP, tokens), lambda c, info: (c, 0, 0))
    return heads, keys, values, inverse


def attention_forward(info, q, kv):
    slots, _, tokens = kv.shape
    heads, keys, values, inverse = attention_specs(slots, tokens)
    return pl.pallas_call(
        forward_kernel,
        grid_spec=pltpu.PrefetchScalarGridSpec(
            num_scalar_prefetch=1,
            grid=(KEY_VALUE_HEADS,),
            in_specs=[heads, keys, values],
            out_specs=[heads, heads, inverse],
        ),
        out_shape=[
            jax.ShapeDtypeStruct((QUERY_WIDTH, tokens), BF),
            jax.ShapeDtypeStruct((QUERY_WIDTH, tokens), F32),
            jax.ShapeDtypeStruct((KEY_VALUE_HEADS, GROUP, tokens), F32),
        ],
        compiler_params=pltpu.CompilerParams(vmem_limit_bytes=48 * 2**20),
        cost_estimate=pl.CostEstimate(flops=0, bytes_accessed=2**20, transcendentals=0),
        name="attention_forward",
    )(info, q, kv, kv)


def attention_backward(info, q, kv, grad, of, inv):
    slots, _, tokens = kv.shape
    heads, keys, values, inverse = attention_specs(slots, tokens)
    return pl.pallas_call(
        backward_kernel,
        grid_spec=pltpu.PrefetchScalarGridSpec(
            num_scalar_prefetch=1,
            grid=(KEY_VALUE_HEADS,),
            in_specs=[heads, keys, values, heads, heads, inverse],
            out_specs=[heads, keys, keys],
        ),
        out_shape=[
            jax.ShapeDtypeStruct((QUERY_WIDTH, tokens), F32),
            jax.ShapeDtypeStruct((slots, KEY_VALUE_WIDTH, tokens), F32),
            jax.ShapeDtypeStruct((slots, KEY_VALUE_WIDTH, tokens), F32),
        ],
        compiler_params=pltpu.CompilerParams(vmem_limit_bytes=48 * 2**20),
        cost_estimate=pl.CostEstimate(flops=0, bytes_accessed=2**20, transcendentals=0),
        name="attention_backward",
    )(info, q, kv, kv, grad, of, inv)


VMEM = 56 * 2**20


def split_kernel(w_ref, gate_ref, up_ref, s_ref):
    rows = gate_ref.shape[0]
    step = w_ref.shape[0] // rows
    s_ref[...] = w_ref[...].astype(F32)
    for c in range(step // 2):
        lanes = slice(c * 128, (c + 1) * 128)
        gate_ref[:, lanes] = s_ref[pl.ds(2 * c, rows, stride=step), :].astype(BF)
        up_ref[:, lanes] = s_ref[pl.ds(2 * c + 1, rows, stride=step), :].astype(BF)


def split_gate_up(w_in):
    units, _, width = w_in.shape
    step = width // 64
    flat = w_in.reshape(units, 2, width // 128, 128).transpose(0, 2, 1, 3)
    flat = flat.reshape(units * step, 128)
    block = 128
    half = pl.BlockSpec((block, width), lambda i: (i, 0))
    return pl.pallas_call(
        split_kernel,
        grid=(units // block,),
        in_specs=[pl.BlockSpec((block * step, 128), lambda i: (i, 0))],
        out_specs=[half, half],
        out_shape=[jax.ShapeDtypeStruct((units, width), BF)] * 2,
        scratch_shapes=[pltpu.VMEM((block * step, 128), F32)],
        compiler_params=pltpu.CompilerParams(vmem_limit_bytes=VMEM),
        cost_estimate=pl.CostEstimate(flops=0, bytes_accessed=2**20, transcendentals=0),
        name="split_gate_up",
    )(flat)


FFN_CUTS = 5


def ffn_kernel(hn_ref, dy_ref, g_hbm, u_hbm, d_hbm, lhs_ref, dhn_ref, out_ref, wg, wu, wd, sems):
    block = wg.shape[0] // FFN_CUTS
    copies = []
    for i in range(FFN_CUTS):
        rows = pl.ds(i * block, block)
        pairs = ((g_hbm, wg), (u_hbm, wu), (d_hbm, wd))
        copies.append(
            [
                pltpu.make_async_copy(src.at[rows], dst.at[rows], sems.at[j, i])
                for j, (src, dst) in enumerate(pairs)
            ]
        )
        for copy in copies[-1]:
            copy.start()
    hn, dy = hn_ref[...], dy_ref[...]
    for i in range(FFN_CUTS):
        for copy in copies[i]:
            copy.wait()
        rows = pl.ds(i * block, block)
        gate = dot(wg[rows, :], hn, 1, 1)
        up = dot(wu[rows, :], hn, 1, 1)
        dm = dot(wd[rows, :], dy, 1, 1)
        sg = 1.0 / (1.0 + jnp.exp(-gate))
        act = gate * sg
        lhs_ref[0, rows, :] = (act * up).astype(BF)
        lhs_ref[1, rows, :] = (dm * up * sg * (1.0 + gate * (1.0 - sg))).astype(BF)
        lhs_ref[2, rows, :] = (dm * act).astype(BF)
    step = 512
    for n in range(wg.shape[1] // step):
        lanes = pl.ds(n * step, step)
        dhn = dot(lhs_ref[1], wg[:, lanes], 0, 0) + dot(lhs_ref[2], wu[:, lanes], 0, 0)
        dhn_ref[:, lanes] = dhn.astype(dhn_ref.dtype)
        out_ref[:, lanes] = dot(lhs_ref[0], wd[:, lanes], 0, 0).astype(out_ref.dtype)


def ffn_slot(hn, dy, w_gate, w_up, w_down, kind):
    tokens, width = hn.shape
    units = w_gate.shape[0]
    whole = pl.BlockSpec(memory_space=pltpu.VMEM)
    far = pl.BlockSpec(memory_space=pl.ANY)
    return pl.pallas_call(
        ffn_kernel,
        in_specs=[whole, whole, far, far, far],
        out_specs=[whole, whole, whole],
        out_shape=[
            jax.ShapeDtypeStruct((3, units, tokens), BF),
            jax.ShapeDtypeStruct((tokens, width), kind),
            jax.ShapeDtypeStruct((tokens, width), kind),
        ],
        scratch_shapes=[pltpu.VMEM((units, width), BF)] * 3
        + [pltpu.SemaphoreType.DMA((3, FFN_CUTS))],
        compiler_params=pltpu.CompilerParams(vmem_limit_bytes=VMEM),
        cost_estimate=pl.CostEstimate(flops=0, bytes_accessed=2**20, transcendentals=0),
        name="ffn_slot",
    )(hn, dy, w_gate, w_up, w_down)


def grad_kernel(slots, *refs):
    left, dy, hn = refs[:slots], refs[slots : 2 * slots], refs[2 * slots : 3 * slots]
    out_ref = refs[-1]
    half = out_ref.shape[1] // 2

    def product(right):
        rows = jnp.concatenate([r[0] for r in left], 1)
        for i in range(2):
            lanes = slice(i * half, (i + 1) * half)
            both = jnp.concatenate([r[:, lanes] for r in right], 0)
            out_ref[:, lanes] = dot(rows, both, 1, 0).astype(BF)

    c = pl.program_id(0)
    pl.when(c == 0)(lambda: product(dy))
    pl.when(c > 0)(lambda: product(hn))


def weight_grads(left, dy, hn):
    slots = len(left)
    _, units, tokens = left[0].shape
    width = dy[0].shape[1]
    cut = units // 2
    lefts = pl.BlockSpec((1, cut, tokens), lambda c, m: (c, m, 0))
    rights = pl.BlockSpec((tokens, width), lambda c, m: (0, 0))
    return pl.pallas_call(
        functools.partial(grad_kernel, slots),
        grid=(3, 2),
        in_specs=[lefts] * slots + [rights] * (2 * slots),
        out_specs=pl.BlockSpec((cut, width), lambda c, m: (2 * c + m, 0)),
        out_shape=jax.ShapeDtypeStruct((3 * units, width), BF),
        compiler_params=pltpu.CompilerParams(vmem_limit_bytes=VMEM),
        cost_estimate=pl.CostEstimate(flops=0, bytes_accessed=2**20, transcendentals=0),
        name="weight_grads",
    )(*left, *dy, *hn)


def widen_kernel(down_ref, gate_ref, up_ref, down_out, in_out):
    down_out[...] = down_ref[...].astype(F32)
    in_out[:, 0, :] = gate_ref[...].astype(F32)
    in_out[:, 1, :] = up_ref[...].astype(F32)


def widen(grads):
    units, width = grads.shape[0] // 3, grads.shape[1]
    block = 128
    blocks = units // block
    return pl.pallas_call(
        widen_kernel,
        grid=(blocks,),
        in_specs=[
            pl.BlockSpec((block, width), lambda i, c=c: (c * blocks + i, 0)) for c in range(3)
        ],
        out_specs=[
            pl.BlockSpec((block, width), lambda i: (i, 0)),
            pl.BlockSpec((block, 2, width), lambda i: (i, 0, 0)),
        ],
        out_shape=[
            jax.ShapeDtypeStruct((units, width), F32),
            jax.ShapeDtypeStruct((units, 2, width), F32),
        ],
        compiler_params=pltpu.CompilerParams(vmem_limit_bytes=VMEM),
        cost_estimate=pl.CostEstimate(flops=0, bytes_accessed=2**20, transcendentals=0),
        name="widen",
    )(grads, grads, grads)


def qkv_grad_kernel(slots, info_ref, *refs):
    xn, dq, dkv = refs[:slots], refs[slots : 2 * slots], refs[2 * slots : 3 * slots]
    away_ref, keep_ref = refs[3 * slots :]
    left = jnp.concatenate([r[...] for r in xn], 0)
    split = dq[0].shape[0]
    i = pl.program_id(0)
    for lanes, grads in ((slice(0, split), dq), (slice(split, None), dkv)):
        product = dot(left, jnp.concatenate([r[...] for r in grads], 1), 0, 1)

        @pl.when(i == 0)
        def _():
            away_ref[:, lanes] = product.astype(BF)

        @pl.when(i == 1)
        def _():
            keep_ref[:, lanes] = product


def qkv_grad(core, xn, dq, dkv):
    slots = len(xn)
    tokens, rows = xn[0].shape
    columns = dq[0].shape[0] + dkv[0].shape[0]
    half = pl.BlockSpec((tokens, rows // 2), lambda i, info: (0, info[0] ^ (1 - i)))
    out = pl.BlockSpec((rows // 2, columns), lambda i, info: (0, 0))
    return pl.pallas_call(
        functools.partial(qkv_grad_kernel, slots),
        grid_spec=pltpu.PrefetchScalarGridSpec(
            num_scalar_prefetch=1,
            grid=(2,),
            in_specs=[half] * slots
            + [pl.BlockSpec(x.shape, lambda i, info: (0, 0)) for x in [*dq, *dkv]],
            out_specs=[out, out],
        ),
        out_shape=[
            jax.ShapeDtypeStruct((rows // 2, columns), BF),
            jax.ShapeDtypeStruct((rows // 2, columns), F32),
        ],
        compiler_params=pltpu.CompilerParams(vmem_limit_bytes=VMEM),
        cost_estimate=pl.CostEstimate(flops=0, bytes_accessed=2**20, transcendentals=0),
        name="qkv_grad",
    )(core.reshape(1).astype(jnp.int32), *xn, *dq, *dkv)


def features_kernel(info_ref, dq_ref, dkv_ref, q_ref, kv_ref, more_q_ref, more_kv_ref, out_ref):
    k = pl.program_id(0)

    @pl.when(k == 0)
    def _():
        out_ref[...] = dot(dq_ref[...], q_ref[...], 0, 1) + dot(dkv_ref[...], kv_ref[...], 0, 1)

    @pl.when(k > 0)
    def _():
        product = dot(dq_ref[...], more_q_ref[0], 0, 1)
        out_ref[...] = product + dot(dkv_ref[...], more_kv_ref[0], 0, 1)


def features_grad(sources, dq, dkv, q, kv, more_q, more_kv):
    rows = q.shape[0]
    tokens = dq.shape[1]
    members = len(sources)
    whole = [pl.BlockSpec(x.shape, lambda k, info: (0, 0)) for x in (dq, dkv, q, kv)]
    more = [
        pl.BlockSpec((1,) + x.shape[1:], lambda k, info: (jnp.maximum(k - 1, 0), 0, 0))
        for x in (more_q, more_kv)
    ]
    return pl.pallas_call(
        features_kernel,
        grid_spec=pltpu.PrefetchScalarGridSpec(
            num_scalar_prefetch=1,
            grid=(members,),
            in_specs=whole + more,
            out_specs=pl.BlockSpec((tokens, rows), lambda k, info: (0, info[k])),
        ),
        out_shape=jax.ShapeDtypeStruct((tokens, rows * members), F32),
        compiler_params=pltpu.CompilerParams(vmem_limit_bytes=VMEM),
        cost_estimate=pl.CostEstimate(flops=0, bytes_accessed=2**20, transcendentals=0),
        name="features_grad",
    )(jnp.stack(sources).astype(jnp.int32), dq, dkv, q, kv, more_q, more_kv)


def inverse_rms(values, axis):
    return lax.rsqrt(jnp.mean(values * values, axis=axis, keepdims=True) + NORM_EPSILON)


def norm_back(grad_out, normed, inv_scale, gain, axis):
    scaled = grad_out * gain
    return inv_scale * (scaled - normed * jnp.mean(scaled * normed, axis=axis, keepdims=True))


def rotate(values, cos_t, sin_t, sign):
    half = HEAD_SIZE // 2
    first, second = values[:, :half], values[:, half:]
    sin_t = sin_t * sign
    return jnp.concatenate([first * cos_t - second * sin_t, second * cos_t + first * sin_t], axis=1)


def per_device(
    layer_input,
    w_qkv,
    w_out,
    w_in,
    w_down,
    attn_gain,
    ffn_gain,
    q_gain,
    k_gain,
    cotangent,
    prefix_len,
    seq_slot,
):
    xf = layer_input[0].astype(F32)
    tokens, width = xf.shape
    g = lax.axis_index("grp")
    core = bit_of(0)
    sources = [from_shift(k) for k in range(lax.axis_size("grp"))]
    positions = g * tokens + jnp.arange(tokens, dtype=jnp.int32)
    slot_ids = jnp.arange(prefix_len.shape[0], dtype=jnp.int32)
    prefix = jnp.sum(jnp.where(slot_ids == seq_slot[0], prefix_len, 0))
    info = jnp.stack([prefix, g * tokens] + [s * tokens for s in sources]).astype(jnp.int32)
    half = HEAD_SIZE // 2
    freqs = ROPE_THETA ** (-(2.0 * jnp.arange(half, dtype=F32)) / HEAD_SIZE)
    angles = freqs[:, None] * positions.astype(F32)[None, :]
    cos_t, sin_t = jnp.cos(angles), jnp.sin(angles)
    w_gate, w_up = split_gate_up(w_in)

    inv_one = inverse_rms(xf, 1)
    normed_one = xf * inv_one
    xn = (normed_one * attn_gain).astype(BF)
    dy = cotangent[0]
    rows = w_qkv.shape[0]
    members = lax.axis_size("grp")

    def project(shards):
        total = 0.0
        for source, shard in shards:
            total = total + dot(
                shard, lax.dynamic_slice_in_dim(xn, source * rows, rows, 1), 0, 1
            )
        return total

    kv_w = Shards(w_qkv[:, QUERY_WIDTH:])
    kv_w.fetch()
    xn, w_qkv, w_out, dy, w_in = hold_with((xn, w_qkv, w_out, dy, w_in), kv_w)
    q_w = Shards(w_qkv[:, :QUERY_WIDTH])
    q_w.fetch()
    kv_w.rest()
    w_out, dy, w_in = hold_with((w_out, dy, w_in), kv_w, q_w)
    kv_w.core()
    kv_t = project(kv_w.shards())
    k_raw = kv_t[:KEY_VALUE_WIDTH].reshape(KEY_VALUE_HEADS, HEAD_SIZE, tokens)
    k_inv = inverse_rms(k_raw, 1)
    k_normed = k_raw * k_inv
    k_low = rotate(k_normed * k_gain[:, None], cos_t, sin_t, 1.0).astype(BF)
    local_kv = jnp.concatenate(
        [k_low.reshape(KEY_VALUE_WIDTH, tokens), kv_t[KEY_VALUE_WIDTH:].astype(BF)], 0
    )
    local_kv, dy, w_in, w_out = hold_with((local_kv, dy, w_in, w_out), q_w)
    kv = [local_kv] + [shift(local_kv, k) for k in range(1, members)]
    q_w.rest()
    w_gate, w_up = split_gate_up(w_in)
    kv, w_gate, w_up, dy, w_out = hold_with((kv, w_gate, w_up, dy, w_out), q_w)
    out_w = Shards(w_out)
    out_w.fetch()
    q_w.core()
    q_t = project(q_w.shards())
    q_raw = q_t.reshape(QUERY_HEADS, HEAD_SIZE, tokens)
    q_inv = inverse_rms(q_raw, 1)
    q_normed = q_raw * q_inv
    q_low = rotate(q_normed * q_gain[:, None], cos_t, sin_t, 1.0).astype(BF)
    q_low = q_low.reshape(QUERY_WIDTH, tokens)
    dy_s = Spread(dy)
    dy_s.hop(1)
    kv, q_low, q_raw = hold_with((kv, q_low, q_raw), out_w, dy_s)
    kv = jnp.stack(kv)

    dy_s.hop(2)
    out_w.rest()
    ob, of, soft_inv = attention_forward(info, q_low, kv)
    ob, of, soft_inv = hold_with((ob, of, soft_inv), out_w, dy_s)
    dy_s.hop(3)
    out_w.core()
    out_shards = out_w.shards()
    hid = xf
    for source, shard in out_shards:
        part = lax.dynamic_slice_in_dim(ob, source * w_out.shape[0], w_out.shape[0], 0)
        hid = hid + dot(part, shard, 0, 0)
    inv_two = inverse_rms(hid, 1)
    normed_two = hid * inv_two
    hn = (normed_two * ffn_gain).astype(BF)
    hn, hid = tie(hn, hid)

    def slot(k):
        kind = F32 if k == 0 else BF
        return ffn_slot(hn_s.slot(k), dy_s.slot(k), w_gate, w_up, w_down, kind)

    hn_s = Spread(hn)
    hn_s.hop(1)
    done = [slot(0)]
    done = hold_with(done, hn_s, dy_s)
    hn_s.hop(2)
    done.append(slot(1))
    done = hold_with(done, hn_s, dy_s)
    hn_s.hop(3)
    done.append(slot(2))
    done = hold_with(done, hn_s)
    dhn_c = Collect([d[1] for d in done])
    dhn_c.parts += [None] * (members - len(dhn_c.parts))
    dhn_c.hop("next")
    done += [slot(k) for k in range(3, members)]
    done = hold_with(done, dhn_c)
    lefts = [d[0] for d in done]
    dhn_c.parts = [d[1] for d in done]
    hn_slots = [hn_s.slot(k) for k in range(members)]
    dy_slots = [dy_s.slot(k) for k in range(members)]
    dhn_c.hop("far")
    dhn_c.hop("next_mid")
    grads = weight_grads(lefts, dy_slots, hn_slots)
    grads = hold_with(grads, dhn_c)
    grads = lax.psum_scatter(grads, "rep", scatter_dimension=0, tiled=True)
    dhn_c.hop("far_mid")
    out_c = Collect([d[2] for d in done])
    out_c.hop("next")
    hold(dhn_c, out_c)
    dhn_c.hop("edge")
    out_c.hop("next_mid")
    xn = hold_with(xn, dhn_c, out_c)

    dhn = dhn_c.result()
    d_ffn_gain = jnp.sum(dhn * normed_two, axis=0)
    dhid = dy.astype(F32) + norm_back(dhn, normed_two, inv_two, ffn_gain, 1)
    dab = dhid.astype(BF)
    dob = jnp.zeros((QUERY_WIDTH, tokens), BF)
    for source, shard in out_shards:
        part = dot(shard, dab, 1, 1).astype(BF)
        dob = lax.dynamic_update_slice_in_dim(dob, part, source * shard.shape[0], 0)

    def out_grad(i):
        half = lax.dynamic_slice_in_dim(dab, i * (width // 2), width // 2, 1)
        return dot(ob, half, 1, 0).reshape(members, w_out.shape[0], width // 2)

    def columns_of(k):
        member = lax.rem(g + k, members)
        return lax.dynamic_slice_in_dim(xn, member * rows, rows, 1)

    xn_slots = [columns_of(0)] + [shift(columns_of(k), k) for k in range(1, members)]

    w_out_r = Reduced(out_grad, 2)
    dob, xn_slots = hold_with((dob, xn_slots), w_out_r)
    w_out_r.core()
    out_c.hop("far")
    dq_rot, dk_part, dv_part = attention_backward(info, q_low, kv, dob, of, soft_inv)
    dkv_part = [jnp.concatenate([dk_part[k], dv_part[k]], 0) for k in range(members)]
    dkv_part = [dkv_part[0]] + [x.astype(BF) for x in dkv_part[1:]]
    dq_rot, dkv_part = hold_with((dq_rot, dkv_part), w_out_r, out_c)
    dkv_c = Direct(dkv_part)
    dq_n = rotate(dq_rot.reshape(QUERY_HEADS, HEAD_SIZE, tokens), cos_t, sin_t, -1.0)
    d_q_gain = jnp.sum(dq_n * q_normed, axis=(0, 2))
    dq = norm_back(dq_n, q_normed, q_inv, q_gain[:, None], 1).reshape(QUERY_WIDTH, tokens)
    dq = dq.astype(BF)
    dq, grads = hold_with((dq, grads), dkv_c)
    grads = lax.all_gather(grads, "rep", axis=0, tiled=True)
    dq_slots = [dq] + [shift(dq, k) for k in range(1, members)]
    w_out_r.rest()
    dkv = dkv_c.result()
    dk_n = rotate(
        dkv[:KEY_VALUE_WIDTH].reshape(KEY_VALUE_HEADS, HEAD_SIZE, tokens), cos_t, sin_t, -1.0
    )
    d_k_gain = jnp.sum(dk_n * k_normed, axis=(0, 2))
    dk = norm_back(dk_n, k_normed, k_inv, k_gain[:, None], 1).reshape(KEY_VALUE_WIDTH, tokens)
    dkv = jnp.concatenate([dk, dkv[KEY_VALUE_WIDTH:]], 0).astype(BF)
    dq_slots, dkv = hold_with((dq_slots, dkv), w_out_r)
    dkv_slots = [dkv] + [shift(dkv, k) for k in range(1, members)]
    w_out_r.members()
    dxn = features_grad(
        sources, dq, dkv, q_w.w, kv_w.w, q_w.whole(), kv_w.whole()
    )
    d_attn_gain = jnp.sum(dxn * normed_one, axis=0)
    input_grad = dhid + norm_back(dxn, normed_one, inv_one, attn_gain, 1)
    gains = jnp.concatenate([d_attn_gain, d_ffn_gain, d_q_gain, d_k_gain])
    dkv_slots, gains, input_grad = hold_with((dkv_slots, gains, input_grad), w_out_r)
    w_out_r.back()
    w_qkv_r = RepSum(*qkv_grad(core, xn_slots, dq_slots, dkv_slots), 0)
    w_qkv_r.core()
    gains = gains + swap(gains, 0)
    gains = hold_with(gains, w_qkv_r, w_out_r)
    w_qkv_r.rest()
    w_out_r.last()
    out_c.hop("far_mid")
    for b in rep_orders()[0][1:]:
        gains = gains + swap(gains, b)
    gains, grads = hold_with((gains, grads), w_qkv_r, w_out_r, out_c)
    w_qkv_r.back()
    d_w_down, d_w_in = widen(grads)
    gains = gains + move(gains, [(i, i ^ 1) for i in range(members)])
    out_c.hop("edge")
    gains, d_w_down, d_w_in = hold_with((gains, d_w_down, d_w_in), w_qkv_r, w_out_r, out_c)
    w_qkv_r.last()
    d_w_out = w_out_r.result()
    for b in range(1, members.bit_length() - 1):
        gains = gains + move(gains, [(i, i ^ (1 << b)) for i in range(members)])
    layer_output = (hid + out_c.result()).astype(BF)
    d_w_out, gains, layer_output = hold_with((d_w_out, gains, layer_output), w_qkv_r)
    d_w_qkv = w_qkv_r.result()
    return (
        layer_output[None],
        input_grad[None],
        d_w_qkv,
        d_w_out,
        d_w_in,
        d_w_down,
        gains[:width],
        gains[width : 2 * width],
        gains[2 * width : 2 * width + HEAD_SIZE],
        gains[2 * width + HEAD_SIZE :],
    )


def solution(mesh):
    in_specs = (
        P("rep", "grp", None),
        P("grp", None),
        P("grp", None),
        P("grp", None, None),
        P("grp", None),
        P(),
        P(),
        P(),
        P(),
        P("rep", "grp", None),
        P(),
        P("rep"),
    )
    out_specs = (
        P("rep", "grp", None),
        P("rep", "grp", None),
        P("grp", None),
        P("grp", None),
        P("grp", None, None),
        P("grp", None),
        P(),
        P(),
        P(),
        P(),
    )
    return jax.shard_map(
        per_device, mesh=mesh, in_specs=in_specs, out_specs=out_specs, check_vma=False
    )
```
